128 devices in a mesh: wide: 32 (over x, z, core), narrow: 4 (over y).
Axes of the slice: x: 4, y: 4, z: 4, core: 2. Of those that a mesh axis runs over, the one named last changes fastest.
Arguments:
- operator_tiles: float32 [32, 4, 32, 8, 128, 128], P('wide', 'narrow')
- tile_slab: int32 [32, 4, 32, 8], P('wide', 'narrow'), may hold values from 0 to 8, as said below
- tile_column: int32 [32, 4, 32, 8], P('wide', 'narrow'), may hold values from 0 to 31, as said below
- tile_live: int32 [32, 4, 32, 8], P('wide', 'narrow'), may hold values from 0 to 1, as said below
- send_list: int32 [32, 4, 16], P('wide', 'narrow'), may hold values from 0 to 31, as said below
- aggregate: int32 [32, 4, 32], P('wide', 'narrow'), may hold values from 0 to 3
- null_modes: float32 [32, 4, 32, 6, 128], P('wide', 'narrow'), may hold values from -0.5 to 0.5
Outputs:
- prolongator: float32 [32, 4, 32, 216, 128], P('wide', 'narrow')
- coarse_operator: float32 [32, 4, 24, 1176], P('wide', 'narrow')
The draws below stay inside these ranges and needn't reach their ends.
Inputs may be any that keep to these rules, and one draw needn't show every extreme that they name: Slot 0 of every block row is its own diagonal block: tile_slab 4, tile_column the row itself, tile_live 1. Every neighbour subdomain named lies inside the mesh. `tile_column`: for tile_slab 4 a block row of the same subdomain; otherwise a position in the neighbour's send_list. `tile_live`: the live tiles of a row are a prefix of its slots; in every subdomain some row uses all 8. `send_list`: distinct block rows of the subdomain.
All inputs are finite; a program needn't handle non-finite values.
Results may differ from the reference program's by a relative error of at most 0.0003.
Values sent between devices are 32-bit elements; how exact they have to be, the bound alone decides.
No kernel may reach another device: no remote copies, remote signals or barrier semaphores. Data moves between devices by JAX's collectives and lax.ppermute only.
A program may use at most 256 MiB of HBM per device.

```python
import math
import jax
import jax.numpy as jnp
import numpy as np
from jax import lax

BS = 128
MODES = 6
R = 32
K = 8
S = 16
AGG = 4
C = 24
SLABS_W = 32
SLABS_N = 4


def tile_lists(key):
    subkeys = jax.random.split(key, 5)
    grid_shape = (SLABS_W, SLABS_N, R, K)
    wide_pos = lax.broadcasted_iota(jnp.int32, grid_shape, 0)
    narrow_pos = lax.broadcasted_iota(jnp.int32, grid_shape, 1)
    row_pos = lax.broadcasted_iota(jnp.int32, grid_shape, 2)
    slot_pos = lax.broadcasted_iota(jnp.int32, grid_shape, 3)
    wide_step = jnp.clip(wide_pos + jax.random.randint(subkeys[0], grid_shape, -1, 2), 0, SLABS_W - 1) - wide_pos
    narrow_step = jnp.clip(narrow_pos + jax.random.randint(subkeys[1], grid_shape, -1, 2), 0, SLABS_N - 1) - narrow_pos
    slab_index = (wide_step + 1) * 3 + narrow_step + 1
    slab_index = jnp.where(slot_pos == 0, 4, slab_index)
    own_column = jax.random.randint(subkeys[2], grid_shape, 0, R)
    far_column = jax.random.randint(subkeys[3], grid_shape, 0, S)
    column = jnp.where(slab_index == 4, own_column, far_column)
    column = jnp.where(slot_pos == 0, row_pos, column)
    used_count = jax.random.randint(subkeys[4], (SLABS_W, SLABS_N, R, 1), 2, K + 1)
    used_count = jnp.where(row_pos[..., :1] == 0, K, used_count)
    live_flags = (slot_pos < used_count).astype(jnp.int32)
    return (slab_index.astype(jnp.int32), column.astype(jnp.int32), live_flags)


def draw_tile_slab(key, part):
    shared = tile_lists(key)
    return shared[0]


def draw_tile_column(key, part):
    shared = tile_lists(key)
    return shared[1]


def draw_tile_live(key, part):
    shared = tile_lists(key)
    return shared[2]


def draw_send_list(key, part):
    key = jax.random.fold_in(key, 4)
    scores = jax.random.randint(key, (SLABS_W, SLABS_N, R), 0, 2 ** 20) * R
    scores = scores + lax.broadcasted_iota(jnp.int32, (SLABS_W, SLABS_N, R), 2)
    order = jnp.argsort(scores, axis=-1, stable=True)
    return order[..., :S].astype(jnp.int32)


def draw_operator_tiles(key, part):
    key = jax.random.fold_in(key, 5)
    subkeys = jax.random.split(key, 3)
    grid_shape = (SLABS_W, SLABS_N, R, K, BS, BS)
    noise = jnp.clip(jax.random.normal(subkeys[0], grid_shape, jnp.float32), -5.0, 5.0)
    row_scale = jnp.exp(jax.random.uniform(subkeys[1], (SLABS_W, SLABS_N, R, K, BS, 1), jnp.float32, math.log(0.5), math.log(2.0)))
    entries = noise * row_scale / math.sqrt(BS * K)
    diag_values = jax.random.uniform(subkeys[2], (SLABS_W, SLABS_N, R, 1, BS, 1), jnp.float32, 1.0, 3.0)
    identity = (lax.broadcasted_iota(jnp.int32, (BS, BS), 0) == lax.broadcasted_iota(jnp.int32, (BS, BS), 1)).astype(jnp.float32)
    first_slot = (lax.broadcasted_iota(jnp.int32, (1, 1, 1, K, 1, 1), 3) == 0).astype(jnp.float32)
    return entries + first_slot * diag_values * identity


def with_ends(array, own_key, low, largest):
    index_at = [jax.random.randint(jax.random.fold_in(own_key, axis), (), 0, length) for axis, length in enumerate(array.shape)]
    main_axis = array.shape.index(max(array.shape))
    beside = index_at[:main_axis] + [(index_at[main_axis] + 1) % array.shape[main_axis]] + index_at[main_axis + 1:]
    return array.at[tuple(index_at)].set(low).at[tuple(beside)].set(largest)


def shard_levels(rng, extent, cuts, low, high):
    factor_of, own = 1.0, jax.random.fold_in(rng, 6)
    for axis_at, blocks in cuts:
        heights = jnp.exp(jax.random.uniform(jax.random.fold_in(own, axis_at), (blocks,), jnp.float32, low / len(cuts), high / len(cuts)))
        factor_of = factor_of * jnp.repeat(heights, extent[axis_at] // blocks).reshape([-1 if axis == axis_at else 1 for axis in range(len(extent))])
    return factor_of


def bell_draw(stream_key, extent, scale, limit, pieces=(), kind=jnp.bfloat16):
    drawn = jax.random.normal(stream_key, extent, jnp.float32) * scale
    if len(pieces) > 0:
        drawn = shard_levels(stream_key, extent, pieces, -0.22, 0.18) * drawn
    return jnp.clip(drawn, min=-limit, max=limit).astype(kind)


def setup_inputs(seed: int = 0) -> dict:
    splits = jax.random.split(jax.random.key(seed), 8)
    operator_tiles = draw_operator_tiles(jax.random.fold_in(splits[7], 71), 0)
    tile_slab = draw_tile_slab(jax.random.fold_in(splits[7], 71), 0)
    tile_column = draw_tile_column(jax.random.fold_in(splits[7], 71), 0)
    tile_live = draw_tile_live(jax.random.fold_in(splits[7], 71), 0)
    send_list = draw_send_list(jax.random.fold_in(splits[7], 71), 0)
    aggregate = with_ends(jax.random.randint(splits[5], (SLABS_W, SLABS_N, R), 0, AGG), jax.random.fold_in(splits[5], 1), 0, AGG - 1).astype(jnp.int32)
    null_modes = bell_draw(splits[6], (SLABS_W, SLABS_N, R, MODES, BS), BS ** -0.5, 0.5, ((0, 32), (1, 4)), jnp.float32)
    return dict(operator_tiles=operator_tiles, tile_slab=tile_slab, tile_column=tile_column, tile_live=tile_live, send_list=send_list, aggregate=aggregate, null_modes=null_modes)


OMEGA = 0.7
HIGH = lax.Precision.HIGHEST


def spread_lookup():
    lookup = np.zeros((9, 9, 25), np.float32)
    for slab_pos in range(9):
        for inner_pos in range(9):
            rowpos = slab_pos // 3 + inner_pos // 3
            colpos = slab_pos % 3 + inner_pos % 3
            lookup[slab_pos, inner_pos, rowpos * 5 + colpos] = 1.0
    return lookup


def owner_lookup():
    lookup = np.zeros((9, 25, 49), np.float32)
    for owner_pos in range(9):
        for target in range(25):
            rowpos = target // 5 - owner_pos // 3 + 2
            colpos = target % 5 - owner_pos % 3 + 2
            lookup[owner_pos, target, rowpos * 7 + colpos] = 1.0
    return lookup


def tentative(null_modes, aggregate):
    member = (aggregate[:, None] == jnp.arange(AGG, dtype=jnp.int32)[None, :]).astype(jnp.float32)
    spread = member[:, :, None, None] * null_modes.astype(jnp.float32)[:, None, :, :]
    return spread.reshape(member.shape[0], AGG * MODES, null_modes.shape[-1])


def smooth(tiles_dev, slab_dev, column_dev, live_dev, tentative_dev, halo_dev):
    block_rows = tentative_dev.shape[0]
    offered = halo_dev.shape[2]
    lookup = jnp.concatenate([tentative_dev, halo_dev.reshape((9 * offered,) + tentative_dev.shape[1:])], 0)
    source_row = jnp.where(slab_dev == 4, column_dev, block_rows + slab_dev * offered + column_dev).astype(jnp.int32)
    operand = lookup[source_row]
    product = jnp.einsum('rkcj,rkij->rkci', operand, tiles_dev, precision=HIGH)
    weights = live_dev.astype(jnp.float32)[..., None] * (slab_dev[..., None] == jnp.arange(9, dtype=jnp.int32)).astype(jnp.float32)
    gathered = jnp.einsum('rkf,rkci->rfci', weights, product, precision=HIGH)
    inverse_diag = 1.0 / jnp.diagonal(tiles_dev[:, 0], axis1=1, axis2=2)
    centered = jnp.zeros(gathered.shape, jnp.float32).at[:, 4].set(tentative_dev)
    return centered - OMEGA * gathered * inverse_diag[:, None, None, :]


def couple(tiles_dev, slab_dev, column_dev, live_dev, prolong_dev, halo_dev):
    block_rows = prolong_dev.shape[0]
    offered = halo_dev.shape[2]
    lookup = jnp.concatenate([prolong_dev, halo_dev.reshape((9 * offered,) + prolong_dev.shape[1:])], 0)
    source_row = jnp.where(slab_dev == 4, column_dev, block_rows + slab_dev * offered + column_dev).astype(jnp.int32)
    operand = lookup[source_row]
    product = jnp.einsum('rkfcj,rkij->rkfci', operand, tiles_dev, precision=HIGH)
    spread = jnp.asarray(spread_lookup(), dtype=jnp.float32)
    weights = live_dev.astype(jnp.float32)[..., None, None] * spread[slab_dev]
    applied = jnp.einsum('rkfe,rkfci->reci', weights, product, precision=HIGH)
    coupled = jnp.einsum('rfci,regi->fceg', prolong_dev, applied, precision=HIGH)
    owners = jnp.asarray(owner_lookup(), dtype=jnp.float32)
    by_owner = jnp.einsum('fceg,feo->fcog', coupled, owners, precision=HIGH)
    width = coupled.shape[1]
    return by_owner.reshape(3, 3, width, 49 * width)


def pad_grid(values):
    return jnp.pad(values, [(1, 1), (1, 1)] + [(0, 0)] * (values.ndim - 2))


def beside_all(padded, wide_pos, narrow_pos):
    zero_start = jnp.zeros((), jnp.int32)
    starts = [jnp.asarray(wide_pos).astype(jnp.int32), jnp.asarray(narrow_pos).astype(jnp.int32)] + [zero_start] * (padded.ndim - 2)
    return lax.dynamic_slice(padded, starts, (3, 3) + padded.shape[2:])


def reference(operator_tiles, tile_slab, tile_column, tile_live, send_list, aggregate, null_modes):
    tent_all = jax.vmap(jax.vmap(tentative))(null_modes, aggregate)
    pick_rows = jax.vmap(jax.vmap(lambda values, rows: values[rows]))
    padded_tent = pad_grid(pick_rows(tent_all, send_list))
    flat_ids = jnp.arange(SLABS_W * SLABS_N, dtype=jnp.int32)

    def first_pass(flat):
        wide_pos = (flat // SLABS_N).astype(jnp.int32)
        narrow_pos = (flat % SLABS_N).astype(jnp.int32)
        return smooth(operator_tiles[wide_pos, narrow_pos], tile_slab[wide_pos, narrow_pos],
                      tile_column[wide_pos, narrow_pos], tile_live[wide_pos, narrow_pos],
                      tent_all[wide_pos, narrow_pos], beside_all(padded_tent, wide_pos, narrow_pos))

    prolong_all = lax.map(first_pass, flat_ids).reshape((SLABS_W, SLABS_N, R, 9, C, BS))
    padded_prolong = pad_grid(pick_rows(prolong_all, send_list))

    def second_pass(flat):
        wide_pos = (flat // SLABS_N).astype(jnp.int32)
        narrow_pos = (flat % SLABS_N).astype(jnp.int32)
        return couple(operator_tiles[wide_pos, narrow_pos], tile_slab[wide_pos, narrow_pos],
                      tile_column[wide_pos, narrow_pos], tile_live[wide_pos, narrow_pos],
                      prolong_all[wide_pos, narrow_pos], beside_all(padded_prolong, wide_pos, narrow_pos))

    owned = lax.map(second_pass, flat_ids).reshape((SLABS_W, SLABS_N, 3, 3, C, 49 * C))
    padded_owned = pad_grid(owned)
    coarse = jnp.zeros((SLABS_W, SLABS_N, C, 49 * C), jnp.float32)
    for wide_off in range(3):
        for narrow_off in range(3):
            coarse = coarse + padded_owned[2 - wide_off:2 - wide_off + SLABS_W, 2 - narrow_off:2 - narrow_off + SLABS_N, wide_off, narrow_off]
    prolongator = prolong_all.reshape((SLABS_W, SLABS_N, R, 9 * C, BS))
    return prolongator, coarse
```

```python
import functools

import jax
import jax.numpy as jnp
from jax import lax
from jax.experimental import pallas as pl
from jax.experimental.pallas import tpu as pltpu
from jax.sharding import PartitionSpec as P

MODES = 6
GROUP = 8
AGG = 4
BS = 128
R = 32
K = 8
S = 16
C = 24
OMEGA = 0.7
E_ROWS = 25 * AGG * GROUP
NT = (((1,), (1,)), ((), ()))
VMEM = pl.BlockSpec(memory_space=pltpu.VMEM)
SMEM = pl.BlockSpec(memory_space=pltpu.SMEM)


def params(mib):
    return pltpu.CompilerParams(vmem_limit_bytes=mib * 2**20)


def split(value):
    high = value.astype(jnp.bfloat16)
    return high, (value - high.astype(jnp.float32)).astype(jnp.bfloat16)


def pair_halo(block, axis, dim):
    size = lax.axis_size(axis)
    near = [(i, i ^ 1) for i in range(size)]
    far = [(i, i + 1) if i % 2 else (i, i - 1) for i in range(1, size - 1)]
    return lax.ppermute(block, axis, near), lax.ppermute(block, axis, far)


def pack_kernel(send, aggregate, modes, own, message):
    for b in range(R):
        for m in range(MODES):
            own[b, m] = modes[m, b]
        own[b, MODES] = jnp.full((BS,), aggregate[b].astype(jnp.float32))
        own[b, MODES + 1] = jnp.zeros((BS,), jnp.float32)
    for s in range(S):
        message[s] = own[send[s]]


def smooth_kernel(send, source, base, live, tiles, table, slots, labels, message):
    eye = lax.broadcasted_iota(jnp.int32, (BS, BS), 0) == lax.broadcasted_iota(
        jnp.int32, (BS, BS), 1
    )
    place = lax.broadcasted_iota(jnp.int32, (GROUP, BS), 0) * BS + lax.broadcasted_iota(
        jnp.int32, (GROUP, BS), 1
    )

    def row(b, marks):
        scale = None
        for k in range(K):
            tile = tiles[b, k]
            if k == 0:
                diagonal = jnp.sum(jnp.where(eye, tile, 0.0), axis=0, keepdims=True)
                scale = OMEGA / diagonal
            modes = table[source[k, b]]
            high, low = split(modes)
            tile_high, tile_low = split(tile)
            left = jnp.concatenate(
                [
                    jnp.concatenate([high, high], 1),
                    jnp.concatenate([low, jnp.zeros_like(low)], 1),
                ],
                0,
            )
            right = jnp.concatenate([tile_high, tile_low], 1)
            both = lax.dot_general(left, right, NT, preferred_element_type=jnp.float32)
            used = live[k, b].astype(jnp.float32)
            value = (both[:GROUP] + both[GROUP:]) * (-scale * used)
            if k == 0:
                value = value + modes
            slots[b, GROUP * k : GROUP * (k + 1)] = value
            mark = modes[MODES : MODES + 1] * float(GROUP) + base[k, b].astype(jnp.float32)
            marks = jnp.where(place == b * K + k, mark, marks)
        return marks

    marks = lax.fori_loop(0, R, row, jnp.zeros((GROUP, BS), jnp.float32))
    labels[...] = marks
    sent = jnp.zeros((GROUP, BS), jnp.float32)
    for s in range(S):
        b = send[s]
        for k in range(K):
            first = (s * K + k) * MODES
            message[first : first + MODES, :] = slots[b, GROUP * k : GROUP * k + MODES]
            mark = table[source[k, b]][MODES : MODES + 1] * float(GROUP) + base[k, b].astype(
                jnp.float32
            )
            sent = jnp.where(place == s * K + k, mark, sent)
    message[S * K * MODES :, :] = sent


def dense_kernel(labels, slots, prolong, lab, wide, sem):
    wide[...] = labels[...].astype(jnp.int32)
    copy = pltpu.make_async_copy(wide, lab, sem)
    copy.start()
    copy.wait()

    def row(b, carry):
        prolong[b] = jnp.zeros((9 * C, BS), jnp.float32)
        for k in range(K):
            flat = b * K + k
            mark = lab[flat // BS, flat % BS]
            e = mark // (AGG * GROUP)
            window = (e // 5) * 3 + e % 5
            member = (mark // GROUP) % AGG
            first = (window * AGG + member) * MODES
            at = pl.ds(first, MODES)
            prolong[b, at, :] += slots[b, GROUP * k : GROUP * k + MODES]
        return carry

    lax.fori_loop(0, R, row, 0)


def couple_kernel(
    where, source, base, live, tiles, slots, labels, prolong, near, left, right,
    own_out, near_out, far_out, table, marks, lab, stage, parts, weights, total, turned, sem
):
    entry_rows = S * K * MODES
    marks[0:2, :] = labels[0:2, :].astype(jnp.int32)
    for block in range(9):
        ref = (near, left, right)[block // 3]
        marks[block + 2 : block + 3, :] = ref[block % 3, entry_rows : entry_rows + 1, :].astype(
            jnp.int32
        )
    copy = pltpu.make_async_copy(marks, lab, sem)
    copy.start()

    def own_entry(b, carry):
        high, low = split(slots[b])
        table[b, :, 0:BS] = high
        table[b, :, BS:] = low
        return carry

    lax.fori_loop(0, R, own_entry, 0)
    stage[...] = jnp.zeros_like(stage)
    for block in range(1, 9):
        ref = (near, left, right)[block // 3]

        def halo_entry(s, carry, block=block, ref=ref):
            rows = ref[block % 3, pl.ds(pl.multiple_of(s * K * MODES, 8), K * MODES), :]
            for g in range(K):
                stage[GROUP * g : GROUP * g + MODES, :] = rows[MODES * g : MODES * (g + 1)]
            high, low = split(stage[...])
            table[R + block * S + s, :, 0:BS] = high
            table[R + block * S + s, :, BS:] = low
            return carry

        lax.fori_loop(0, S, halo_entry, 0)

    total[...] = jnp.zeros_like(total)
    weights[...] = jnp.zeros_like(weights)
    copy.wait()

    def row(b, carry):
        high, low = split(prolong[b])
        weights[0 : 9 * C, 0:BS] = high
        weights[0 : 9 * C, BS : 2 * BS] = high
        weights[0 : 9 * C, 2 * BS :] = low
        for k in range(K):
            entry = table[source[k, b]]
            high, low = entry[:, :BS], entry[:, BS:]
            lhs = jnp.concatenate(
                [
                    jnp.concatenate([high, high], 1),
                    jnp.concatenate([low, jnp.zeros_like(low)], 1),
                ],
                0,
            )
            tile_high, tile_low = split(tiles[b, k])
            rhs = jnp.concatenate([tile_high, tile_low], 1)
            both = lax.dot_general(lhs, rhs, NT, preferred_element_type=jnp.float32)
            used = live[k, b].astype(jnp.float32)
            value = (both[: K * GROUP] + both[K * GROUP :]) * used
            high, low = split(value)
            parts[K * GROUP * k : K * GROUP * (k + 1), :] = jnp.concatenate([high, low, high], 1)
        product = lax.dot_general(
            parts[...], weights[...], NT, preferred_element_type=jnp.float32
        )
        for k in range(K):
            src = source[k, b]
            major, minor = src // S, (src % S) * K
            shift = base[k, b]
            for g in range(K):
                first = pl.multiple_of(lab[major, minor + g] + shift, GROUP)
                at = (K * k + g) * GROUP
                total[pl.ds(first, GROUP), :] += product[at : at + GROUP]
        return carry

    lax.fori_loop(0, R, row, 0)
    for g in range(25 * AGG):
        turned[MODES * g : MODES * (g + 1), :] = total[GROUP * g : GROUP * g + MODES, :]
    flat = turned[...].T
    even = where[0] == 0
    low, mid, top = (flat[3 * C * i : 3 * C * (i + 1)] for i in range(3))
    own_out[...] = mid
    near_out[...] = jnp.where(even, top, low)
    far_out[...] = jnp.where(even, low, top)


def merge_kernel(where, own, near, far, own_out, near_out, far_out):
    even = where[0] == 0
    span = 5 * C
    low = jnp.where(even, near[...], far[...])
    top = jnp.where(even, far[...], near[...])
    zeros = jnp.zeros((3 * C, span), jnp.float32)
    mid = own[...]
    length = 5 * span
    summed = (
        jnp.concatenate([top[:, :length], zeros, zeros], 1)
        + jnp.concatenate([zeros, mid[:, :length], zeros], 1)
        + jnp.concatenate([zeros, zeros, low[:, :length]], 1)
    )
    even = where[1] == 0
    low, mid, top = (summed[C * i : C * (i + 1)] for i in range(3))
    own_out[...] = mid
    near_out[...] = jnp.where(even, top, low)
    far_out[...] = jnp.where(even, low, top)


def place_kernel(where, own, near, far, coarse):
    even = where[1] == 0
    low = jnp.where(even, near[...], far[...])
    top = jnp.where(even, far[...], near[...])
    mid = own[...]
    zeros = jnp.zeros((C, C), jnp.float32)
    pieces = []
    for u in range(7):
        lanes = slice(5 * C * u, 5 * C * (u + 1))
        pieces.append(
            jnp.concatenate([top[:, lanes], zeros, zeros], 1)
            + jnp.concatenate([zeros, mid[:, lanes], zeros], 1)
            + jnp.concatenate([zeros, zeros, low[:, lanes]], 1)
        )
    coarse[...] = jnp.concatenate(pieces, 1)


def shape(*dims, dtype=jnp.float32):
    return jax.ShapeDtypeStruct(dims, dtype)


def body(operator_tiles, tile_slab, tile_column, tile_live, send_list, aggregate, null_modes):
    tiles = operator_tiles[0, 0]
    slab = tile_slab[0, 0].T
    column = tile_column[0, 0].T
    live = tile_live[0, 0].T
    send = send_list[0, 0]
    wide_odd = lax.axis_index("wide") % 2
    narrow_odd = lax.axis_index("narrow") % 2
    where = jnp.stack([wide_odd, narrow_odd]).astype(jnp.int32)
    down, across = slab // 3 - 1, slab % 3 - 1
    near_down, near_across = 1 - 2 * wide_odd, 1 - 2 * narrow_odd
    row_block = jnp.where(down == 0, 0, jnp.where(down == near_down, 1, 2))
    col_block = jnp.where(across == 0, 0, jnp.where(across == near_across, 1, 2))
    source = jnp.where(slab == 4, column, R + (row_block * 3 + col_block) * S + column)
    base = (5 * (slab // 3) + slab % 3) * (AGG * GROUP)

    own_modes, packed = pl.pallas_call(
        pack_kernel,
        out_shape=(shape(R, GROUP, BS), shape(S, GROUP, BS)),
        in_specs=[SMEM, SMEM, VMEM],
        out_specs=(VMEM, VMEM),
        name="pack",
    )(send, aggregate[0, 0], null_modes[0, 0].transpose(1, 0, 2))
    near, far = pair_halo(packed, "narrow", 0)
    line = jnp.concatenate([packed, near, far], 0)
    near, far = pair_halo(line, "wide", 0)
    table = jnp.concatenate([own_modes, line, near, far], 0)

    slots, labels, message = pl.pallas_call(
        smooth_kernel,
        out_shape=(
            shape(R, K * GROUP, BS),
            shape(GROUP, BS),
            shape(S * K * MODES + GROUP, BS),
        ),
        in_specs=[SMEM] * 4 + [VMEM] * 2,
        out_specs=(VMEM, VMEM, VMEM),
        compiler_params=params(32),
        name="smooth",
    )(send, source, base, live, tiles, table)

    message = message[None]
    near, far = pair_halo(message, "narrow", 0)
    prolong = pl.pallas_call(
        dense_kernel,
        out_shape=shape(R, 9 * C, BS),
        in_specs=[VMEM, VMEM],
        out_specs=VMEM,
        scratch_shapes=[
            pltpu.SMEM((GROUP, BS), jnp.int32),
            pltpu.VMEM((GROUP, BS), jnp.int32),
            pltpu.SemaphoreType.DMA,
        ],
        compiler_params=params(16),
        name="dense",
    )(labels, slots)
    line = jnp.concatenate([message, near, far], 0)
    near, far = pair_halo(line, "wide", 0)

    rows = 3 * C
    lanes = 25 * C
    own, near, far = pl.pallas_call(
        couple_kernel,
        out_shape=(shape(rows, lanes),) * 3,
        in_specs=[SMEM] * 4 + [VMEM] * 7,
        out_specs=(VMEM,) * 3,
        scratch_shapes=[
            pltpu.VMEM((R + 9 * S, K * GROUP, 2 * BS), jnp.bfloat16),
            pltpu.VMEM((16, BS), jnp.int32),
            pltpu.SMEM((16, BS), jnp.int32),
            pltpu.VMEM((K * GROUP, BS), jnp.float32),
            pltpu.VMEM((K * K * GROUP, 3 * BS), jnp.bfloat16),
            pltpu.VMEM((256, 3 * BS), jnp.bfloat16),
            pltpu.VMEM((E_ROWS, 256), jnp.float32),
            pltpu.VMEM((25 * C, 256), jnp.float32),
            pltpu.SemaphoreType.DMA,
        ],
        compiler_params=params(48),
        name="couple",
    )(where, source, base, live, tiles, slots, labels, prolong, line, near, far)

    size = lax.axis_size("wide")
    pairs = [(i, i ^ 1) for i in range(size)]
    far_pairs = [(i, i + 1) if i % 2 else (i, i - 1) for i in range(1, size - 1)]
    near, far = lax.ppermute(near, "wide", pairs), lax.ppermute(far, "wide", far_pairs)
    own, near, far = pl.pallas_call(
        merge_kernel,
        out_shape=(shape(C, 35 * C),) * 3,
        in_specs=[SMEM] + [VMEM] * 3,
        out_specs=(VMEM,) * 3,
        name="merge",
    )(where, own, near, far)
    size = lax.axis_size("narrow")
    pairs = [(i, i ^ 1) for i in range(size)]
    far_pairs = [(i, i + 1) if i % 2 else (i, i - 1) for i in range(1, size - 1)]
    near, far = lax.ppermute(near, "narrow", pairs), lax.ppermute(far, "narrow", far_pairs)
    coarse = pl.pallas_call(
        place_kernel,
        out_shape=shape(C, 49 * C),
        in_specs=[SMEM] + [VMEM] * 3,
        out_specs=VMEM,
        name="place",
    )(where, own, near, far)
    return prolong[None, None], coarse[None, None]


def solution(mesh):
    in_specs = (
        P("wide", "narrow", None, None, None, None),
        P("wide", "narrow", None, None),
        P("wide", "narrow", None, None),
        P("wide", "narrow", None, None),
        P("wide", "narrow", None),
        P("wide", "narrow", None),
        P("wide", "narrow", None, None, None),
    )
    out_specs = (P("wide", "narrow", None, None, None), P("wide", "narrow", None, None))
    return jax.shard_map(body, mesh=mesh, in_specs=in_specs, out_specs=out_specs, check_vma=False)
```

```python
import functools

import jax
import jax.numpy as jnp
from jax import lax
from jax.experimental import pallas as pl
from jax.experimental.pallas import tpu as pltpu
from jax.sharding import PartitionSpec as P

MODES = 6
GROUP = 8
AGG = 4
BS = 128
R = 32
K = 8
S = 16
C = 24
OMEGA = 0.7
UNROLL = 16
BLOCK = S * K * MODES + GROUP
T_ENTRIES = R + 8 * S
NT = (((1,), (1,)), ((), ()))
VMEM = pl.BlockSpec(memory_space=pltpu.VMEM)
SMEM = pl.BlockSpec(memory_space=pltpu.SMEM)
HBM = pl.BlockSpec(memory_space=pltpu.HBM)


def params(mib):
    return pltpu.CompilerParams(vmem_limit_bytes=mib * 2**20)


def split(value):
    high = value.astype(jnp.bfloat16)
    return high, (value - high.astype(jnp.float32)).astype(jnp.bfloat16)


def pair_halo(block, axis, dim):
    size = lax.axis_size(axis)
    near = [(i, i ^ 1) for i in range(size)]
    far = [(i, i + 1) if i % 2 else (i, i - 1) for i in range(1, size - 1)]
    return lax.ppermute(block, axis, near), lax.ppermute(block, axis, far)


def pack_kernel(send_hbm, aggregate_hbm, modes_hbm, own, message, send, aggregate, modes, sems):
    copies = [
        pltpu.make_async_copy(source, target, sems.at[i])
        for i, (source, target) in enumerate(
            ((modes_hbm, modes), (aggregate_hbm, aggregate), (send_hbm, send))
        )
    ]
    for copy in copies:
        copy.start()
    for copy in copies:
        copy.wait()
    for b in range(R):
        for m in range(MODES):
            own[b, m] = modes[m, b]
        own[b, MODES] = jnp.full((BS,), aggregate[b].astype(jnp.float32))
        own[b, MODES + 1] = jnp.zeros((BS,), jnp.float32)
    for s in range(S):
        message[s] = own[send[s]]


def pair_rows(high, low):
    zero = jnp.zeros_like(low)
    return jnp.concatenate(
        [jnp.concatenate([high, high], 1), jnp.concatenate([low, zero], 1)], 0
    )


def times_tile(value, tile):
    length = value.shape[0]
    both = lax.dot_general(
        pair_rows(*split(value)),
        jnp.concatenate(split(tile), 1),
        NT,
        preferred_element_type=jnp.float32,
    )
    return both[:length] + both[length:]


def scale_of(tile):
    eye = lax.broadcasted_iota(jnp.int32, (BS, BS), 0) == lax.broadcasted_iota(
        jnp.int32, (BS, BS), 1
    )
    diagonal = jnp.sum(jnp.where(eye, tile, 0.0), axis=0, keepdims=True)
    return jnp.broadcast_to(-OMEGA / diagonal, (GROUP, BS))


def member_marks(ints, table):
    source = (ints[0:K, :] >> 8) & 255

    def some(i, marks):
        for j in range(8):
            at = i * 8 + j
            marks = jnp.where(source == at, table[at, MODES : MODES + 1, :], marks)
        return marks

    return lax.fori_loop(0, T_ENTRIES // 8, some, jnp.zeros((K, BS), jnp.float32))


def coarse_marks(ints, members):
    return members + (((ints[0:K, :] >> 16) & 31) * AGG).astype(jnp.float32)


def live_of(entry):
    return (((entry >> 21) & 3) != 0).astype(jnp.int32)


def fetch(tiles, entry, taken, at, sems):
    return pltpu.make_async_copy(tiles.at[entry & 255], taken.at[at], sems.at[at])


def start_tiles(rows, scalars, tiles, work, taken, sems):
    for s in range(S):
        work[s] = scalars[0, rows(s)]
        fetch(tiles, work[s], taken, s, sems).start()

    def row(s, count):
        b = rows(s)
        for k in range(1, K):
            entry = scalars[k, b]
            work[count] = entry
            live = live_of(entry)

            @pl.when(live != 0)
            def _(entry=entry, count=count):
                fetch(tiles, entry, taken, count, sems).start()

            count = count + live
        return count

    return lax.fori_loop(0, S, row, S)


def smooth_tiles(count, tiles, table, slots, scale, work, taken, sems):
    for s in range(S):
        fetch(tiles, work[s], taken, s, sems).wait()
    for s in range(S):
        entry = work[s]
        at = entry & 255
        tile = taken[s]
        modes = table[(entry >> 8) & 255]
        factor = scale_of(tile)
        scale[at // K] = factor
        slots[at] = times_tile(modes, tile) * factor + modes

    def some(i, carry):
        for j in range(UNROLL):
            at = i * UNROLL + j

            @pl.when(at < count)
            def _(at=at):
                fetch(tiles, work[at], taken, at, sems).wait()

        for j in range(UNROLL):
            place = jnp.minimum(i * UNROLL + j, count - 1)
            entry = work[place]
            at = entry & 255
            value = times_tile(table[(entry >> 8) & 255], taken[place])
            slots[at] = value * scale[at // K]
        return carry

    lax.fori_loop(1, (count + UNROLL - 1) // UNROLL, some, 0)


def offer_kernel(scalars, ints, tiles, table, slots, message, scale, work, taken, sems):
    count = start_tiles(lambda s: scalars[K, s], scalars, tiles, work, taken, sems)
    slots[...] = jnp.zeros_like(slots)
    marks = coarse_marks(ints, member_marks(ints, table))
    chosen = lax.broadcasted_iota(jnp.int32, (BS, BS), 0) == ints[K : K + 1, :]
    message[S * K * MODES :, :] = jnp.dot(
        marks, chosen.astype(jnp.float32), preferred_element_type=jnp.float32
    )
    smooth_tiles(count, tiles, table, slots, scale, work, taken, sems)
    for s in range(S):
        b = scalars[K, s]
        for k in range(K):
            first = (s * K + k) * MODES
            message[first : first + MODES, :] = slots[b * K + k, :MODES]


def rest_kernel(
    scalars, ints, tiles, table, begun, prolong_hbm, blocks, weights,
    prolong, slots, scale, work, rest, flags, marks, lab, dense_even, dense_odd, taken, sem, sems, tile_sems
):
    for b in range(R):
        flags[b] = 0
    for s in range(S):
        flags[scalars[K, s]] = 1
    count = 0
    for b in range(R):
        rest[count] = b
        count = count + 1 - flags[b]
    count = start_tiles(lambda s: rest[s], scalars, tiles, work, taken, tile_sems)
    members = member_marks(ints, table)
    coarse = coarse_marks(ints, members)
    blocks[S * K * MODES : BLOCK, :] = coarse
    blocks[BLOCK + S * K * MODES :, :] = jnp.concatenate([coarse[:, S:], coarse[:, :S]], 1)
    marks[...] = members.astype(jnp.int32) + ((ints[0:K, :] >> 23) & 15) * AGG
    copy = pltpu.make_async_copy(marks, lab, sem)
    copy.start()
    slots[...] = begun[...]
    smooth_tiles(count, tiles, table, slots, scale, work, taken, tile_sems)
    copy.wait()

    def send_row(b):
        return pltpu.make_async_copy(prolong.at[b], prolong_hbm.at[b], sems.at[b])

    def rows(i, carry):
        for j, dense in enumerate((dense_even, dense_odd)):
            b = i * 2 + j
            dense[...] = jnp.zeros_like(dense)
            for k in range(K):
                dense[lab[k, b]] += slots[b * K + k]
            for g in range(9 * AGG):
                prolong[b, MODES * g : MODES * (g + 1), :] = dense[g, :MODES]
            block, place = b // S, b % S
            start = pl.multiple_of(block * BLOCK + place * K * MODES, GROUP)
            own = jnp.concatenate([slots[b * K + k, :MODES] for k in range(K)], 0)
            blocks[pl.ds(start, K * MODES), :] = own
            high, low = split(prolong[b])
            weights[b, 0 : 9 * C, 0:BS] = high
            weights[b, 0 : 9 * C, BS:] = low
        for j in range(2):
            send_row(i * 2 + j).start()
        return carry

    lax.fori_loop(0, R // 2, rows, 0)

    def finish(b, carry):
        send_row(b).wait()
        return carry

    lax.fori_loop(0, R, finish, 0)


def couple_tiles(
    kind, first_block, scalars, tiles, weights, table, marks, lab, work, parts, products, total, sem
):
    for i in range(table.shape[0] // BLOCK):
        first = i * BLOCK + S * K * MODES
        marks[i * K : (i + 1) * K, :] = table[first : first + K, :].astype(jnp.int32)
    copy = pltpu.make_async_copy(marks, lab, sem)
    copy.start()
    dummy = (25 << 16) + (first_block * S << 8)
    ahead = 2 * UNROLL
    for j in range(ahead):
        work[j] = dummy

    def row(b, count):
        for k in range(K):
            entry = scalars[k, b]
            work[count] = entry
            count = count + (((entry >> 21) & 3) == kind).astype(jnp.int32)
        work[count] = dummy + b * K
        return count + (count & 1)

    count = lax.fori_loop(0, R, row, ahead)
    for j in range(3 * UNROLL):
        work[count + j] = dummy
    length = K * MODES
    copy.wait()

    def step(i, carry):
        start = i * UNROLL
        for j in range(UNROLL):
            entry = work[start + j]
            source = (entry >> 8) & 255
            shift = ((entry >> 16) & 31) * AGG
            major, minor = ((source >> 4) - first_block) * K, source & 15
            for g in range(K):
                at = (K * j + g) * MODES
                total[lab[major + g, minor] + shift] += products[at : at + GROUP, :]
        for j in range(0, UNROLL, 2):
            b = (work[start + UNROLL + j] & 255) // K
            both = weights[b]
            at = slice(j * length, (j + 2) * length)
            products[at, :] = lax.dot_general(
                parts[at, :],
                jnp.concatenate([both[:, :BS], both], 1),
                NT,
                preferred_element_type=jnp.float32,
            )
        for j in range(UNROLL):
            entry = work[start + ahead + j]
            source = (entry >> 8) & 255
            first = ((source >> 4) - first_block) * BLOCK + (source & 15) * length
            rows = table[pl.ds(pl.multiple_of(first, GROUP), length), :]
            high, low = split(times_tile(rows, tiles[entry & 255]))
            parts[length * j : length * (j + 1), :] = jnp.concatenate([high, low, high], 1)
        return carry

    lax.fori_loop(0, (count - ahead + UNROLL - 1) // UNROLL + 2, step, 0)


def beside_kernel(
    scalars, tiles, weights, table, out, marks, lab, work, parts, products, total, sem
):
    total[0 : 25 * AGG] = jnp.zeros((25 * AGG, GROUP, 256), jnp.float32)
    couple_tiles(
        1, 0, scalars, tiles, weights, table, marks, lab, work, parts, products, total, sem
    )
    out[...] = total[0 : 25 * AGG]


def corner_kernel(
    scalars, tiles, weights, begun, table, own_out, near_out, far_out,
    marks, lab, work, parts, products, total, turned, sem
):
    total[0 : 25 * AGG] = begun[...]
    couple_tiles(
        2, 7, scalars, tiles, weights, table, marks, lab, work, parts, products, total, sem
    )
    for g in range(25 * AGG):
        turned[MODES * g : MODES * (g + 1), :] = total[g, :MODES, :]
    flat = turned[...].T
    even = scalars[K + 1, 0] == 0
    low, mid, top = (flat[3 * C * i : 3 * C * (i + 1)] for i in range(3))
    own_out[...] = mid
    near_out[...] = jnp.where(even, top, low)
    far_out[...] = jnp.where(even, low, top)


def merge_kernel(where, own, near, far, own_out, near_out, far_out):
    even = where[K + 1, 0] == 0
    span = 5 * C
    low = jnp.where(even, near[...], far[...])
    top = jnp.where(even, far[...], near[...])
    zeros = jnp.zeros((3 * C, span), jnp.float32)
    mid = own[...]
    length = 5 * span
    summed = (
        jnp.concatenate([top[:, :length], zeros, zeros], 1)
        + jnp.concatenate([zeros, mid[:, :length], zeros], 1)
        + jnp.concatenate([zeros, zeros, low[:, :length]], 1)
    )
    even = where[K + 1, 1] == 0
    low, mid, top = (summed[C * i : C * (i + 1)] for i in range(3))
    own_out[...] = mid
    near_out[...] = jnp.where(even, top, low)
    far_out[...] = jnp.where(even, low, top)


def place_kernel(where, own, near, far, coarse):
    even = where[K + 1, 1] == 0
    low = jnp.where(even, near[...], far[...])
    top = jnp.where(even, far[...], near[...])
    mid = own[...]
    zeros = jnp.zeros((C, C), jnp.float32)
    pieces = []
    for u in range(7):
        lanes = slice(5 * C * u, 5 * C * (u + 1))
        pieces.append(
            jnp.concatenate([top[:, lanes], zeros, zeros], 1)
            + jnp.concatenate([zeros, mid[:, lanes], zeros], 1)
            + jnp.concatenate([zeros, zeros, low[:, lanes]], 1)
        )
    coarse[...] = jnp.concatenate(pieces, 1)


def shape(*dims, dtype=jnp.float32):
    return jax.ShapeDtypeStruct(dims, dtype)


def body(operator_tiles, tile_slab, tile_column, tile_live, send_list, aggregate, null_modes):
    tiles = operator_tiles[0, 0]
    slab = tile_slab[0, 0].T
    column = tile_column[0, 0].T
    live = tile_live[0, 0].T
    send = send_list[0, 0]
    wide_odd = lax.axis_index("wide") % 2
    narrow_odd = lax.axis_index("narrow") % 2
    down, across = slab // 3 - 1, slab % 3 - 1
    row_block = jnp.where(down == 0, 0, jnp.where(down == 1 - 2 * wide_odd, 1, 2))
    col_block = jnp.where(across == 0, 0, jnp.where(across == 1 - 2 * narrow_odd, 1, 2))
    block = 1 + 3 * row_block + col_block
    source = jnp.where(slab == 4, column, block * S + column)
    kind = jnp.where(live == 0, 0, jnp.where(row_block == 2, 2, 1))
    place = lax.broadcasted_iota(jnp.int32, (K, R), 1) * K + lax.broadcasted_iota(
        jnp.int32, (K, R), 0
    )
    entries = (
        place
        + (source << 8)
        + ((5 * (slab // 3) + slab % 3) << 16)
        + (kind << 21)
        + (slab << 23)
    )
    lanes = lax.broadcasted_iota(jnp.int32, (1, BS), 1)
    parity = jnp.where(lanes == 0, wide_odd, narrow_odd).astype(jnp.int32)
    scalars = jnp.concatenate(
        [
            jnp.pad(entries, ((0, 0), (0, BS - R))),
            jnp.pad(send[None], ((0, 0), (0, BS - S))),
            parity,
            jnp.zeros((6, BS), jnp.int32),
        ],
        0,
    )

    own_modes, offered = pl.pallas_call(
        pack_kernel,
        out_shape=(shape(R, GROUP, BS), shape(S, GROUP, BS)),
        in_specs=[HBM] * 3,
        out_specs=(VMEM, VMEM),
        scratch_shapes=[
            pltpu.SMEM((S,), jnp.int32),
            pltpu.SMEM((R,), jnp.int32),
            pltpu.VMEM((MODES, R, BS), jnp.float32),
            pltpu.SemaphoreType.DMA((3,)),
        ],
        compiler_params=params(4),
        name="pack",
    )(
        *(
            pltpu.with_memory_space_constraint(x, pltpu.HBM)
            for x in (send, aggregate[0, 0], null_modes[0, 0].transpose(1, 0, 2))
        )
    )
    near, far = pair_halo(offered, "narrow", 0)
    line = jnp.concatenate([offered, near, far], 0)
    wide_near, wide_far = pair_halo(line, "wide", 0)
    table = jnp.concatenate([own_modes, near, far, wide_near, wide_far], 0)

    tiles = tiles.reshape(R * K, BS, BS)
    resting = pltpu.with_memory_space_constraint(tiles, pltpu.HBM)
    listed = pltpu.SMEM((400,), jnp.int32)
    taken = pltpu.VMEM((S * K, BS, BS), jnp.float32)
    scales = pltpu.VMEM((R, GROUP, BS), jnp.float32)
    begun, message = pl.pallas_call(
        offer_kernel,
        out_shape=(shape(R * K, GROUP, BS), shape(BLOCK, BS)),
        in_specs=[SMEM, VMEM, HBM, VMEM],
        out_specs=(VMEM, VMEM),
        scratch_shapes=[
            scales,
            listed,
            taken,
            pltpu.SemaphoreType.DMA((S * K,)),
        ],
        compiler_params=params(16),
        name="offer",
    )(scalars, scalars, resting, table)

    narrow_near, narrow_far = pair_halo(message, "narrow", 0)
    prolong, blocks, weights = pl.pallas_call(
        rest_kernel,
        out_shape=(
            shape(R, 9 * C, BS),
            shape(2 * BLOCK, BS),
            shape(R, 256, 2 * BS, dtype=jnp.bfloat16),
        ),
        in_specs=[SMEM, VMEM, HBM, VMEM, VMEM],
        out_specs=(HBM, VMEM, VMEM),
        scratch_shapes=[
            pltpu.VMEM((R, 9 * C, BS), jnp.float32),
            pltpu.VMEM((R * K, GROUP, BS), jnp.float32),
            scales,
            listed,
            pltpu.SMEM((R + 8,), jnp.int32),
            pltpu.SMEM((R,), jnp.int32),
            pltpu.VMEM((K, BS), jnp.int32),
            pltpu.SMEM((K, BS), jnp.int32),
            pltpu.VMEM((9 * AGG, GROUP, BS), jnp.float32),
            pltpu.VMEM((9 * AGG, GROUP, BS), jnp.float32),
            taken,
            pltpu.SemaphoreType.DMA,
            pltpu.SemaphoreType.DMA((R,)),
            pltpu.SemaphoreType.DMA((S * K,)),
        ],
        compiler_params=params(24),
        cost_estimate=pl.CostEstimate(flops=2 * 10**9, bytes_accessed=2 * 10**7, transcendentals=0),
        name="rest",
    )(scalars, scalars, resting, table, begun)
    line = jnp.concatenate([message, narrow_near, narrow_far], 0)
    line, weights = lax.optimization_barrier((line, weights))
    wide_near, wide_far = pair_halo(line, "wide", 0)

    def coupling(blocks):
        return [
            pltpu.VMEM((blocks * K, BS), jnp.int32),
            pltpu.SMEM((blocks * K, BS), jnp.int32),
            listed,
            pltpu.VMEM((UNROLL * K * MODES, 3 * BS), jnp.bfloat16),
            pltpu.VMEM((UNROLL * K * MODES + GROUP, 256), jnp.float32),
            pltpu.VMEM((25 * AGG + 52, GROUP, 256), jnp.float32),
        ]

    table = jnp.concatenate([blocks, narrow_near, narrow_far, wide_near], 0)
    total = pl.pallas_call(
        beside_kernel,
        out_shape=shape(25 * AGG, GROUP, 256),
        in_specs=[SMEM] + [VMEM] * 3,
        out_specs=VMEM,
        scratch_shapes=coupling(7) + [pltpu.SemaphoreType.DMA],
        compiler_params=params(16),
        cost_estimate=pl.CostEstimate(flops=8 * 10**9, bytes_accessed=3 * 10**7, transcendentals=0),
        name="beside",
    )(scalars, tiles, weights, table)
    own, near, far = pl.pallas_call(
        corner_kernel,
        out_shape=(shape(3 * C, 25 * C),) * 3,
        in_specs=[SMEM] + [VMEM] * 4,
        out_specs=(VMEM,) * 3,
        scratch_shapes=coupling(3)
        + [pltpu.VMEM((25 * C, 256), jnp.float32), pltpu.SemaphoreType.DMA],
        compiler_params=params(16),
        name="corner",
    )(scalars, tiles, weights, total, wide_far)

    size = lax.axis_size("wide")
    pairs = [(i, i ^ 1) for i in range(size)]
    far_pairs = [(i, i + 1) if i % 2 else (i, i - 1) for i in range(1, size - 1)]
    near, far = lax.ppermute(near, "wide", pairs), lax.ppermute(far, "wide", far_pairs)
    own, near, far = pl.pallas_call(
        merge_kernel,
        out_shape=(shape(C, 35 * C),) * 3,
        in_specs=[SMEM] + [VMEM] * 3,
        out_specs=(VMEM,) * 3,
        compiler_params=params(4),
        name="merge",
    )(scalars, own, near, far)
    size = lax.axis_size("narrow")
    pairs = [(i, i ^ 1) for i in range(size)]
    far_pairs = [(i, i + 1) if i % 2 else (i, i - 1) for i in range(1, size - 1)]
    near, far = lax.ppermute(near, "narrow", pairs), lax.ppermute(far, "narrow", far_pairs)
    coarse = pl.pallas_call(
        place_kernel,
        out_shape=shape(C, 49 * C),
        in_specs=[SMEM] + [VMEM] * 3,
        out_specs=VMEM,
        compiler_params=params(4),
        name="place",
    )(scalars, own, near, far)
    return prolong[None, None], coarse[None, None]


def solution(mesh):
    in_specs = (
        P("wide", "narrow", None, None, None, None),
        P("wide", "narrow", None, None),
        P("wide", "narrow", None, None),
        P("wide", "narrow", None, None),
        P("wide", "narrow", None),
        P("wide", "narrow", None),
        P("wide", "narrow", None, None, None),
    )
    out_specs = (P("wide", "narrow", None, None, None), P("wide", "narrow", None, None))
    return jax.shard_map(body, mesh=mesh, in_specs=in_specs, out_specs=out_specs, check_vma=False)
```

```python
import functools

import jax
import jax.numpy as jnp
from jax import lax
from jax.experimental import pallas as pl
from jax.experimental.pallas import tpu as pltpu
from jax.sharding import PartitionSpec as P

MODES = 6
GROUP = 8
AGG = 4
BS = 128
R = 32
K = 8
S = 16
C = 24
OMEGA = 0.7
BLOCK = S * K * MODES + GROUP
T_ENTRIES = R + 8 * S
UNROLL = 16
SMOOTH = 32
LIST = 384
LISTS = K + 2
NT = (((1,), (1,)), ((), ()))
VMEM = pl.BlockSpec(memory_space=pltpu.VMEM)
SMEM = pl.BlockSpec(memory_space=pltpu.SMEM)
HBM = pl.BlockSpec(memory_space=pltpu.HBM)


def params(mib):
    return pltpu.CompilerParams(vmem_limit_bytes=mib * 2**20)


def split(value):
    high = value.astype(jnp.bfloat16)
    return high, (value - high.astype(jnp.float32)).astype(jnp.bfloat16)


def pair_near(block, axis):
    return lax.ppermute(block, axis, [(i, i ^ 1) for i in range(lax.axis_size(axis))])


def pair_far(block, axis):
    pairs = [(i, i + 1) if i % 2 else (i, i - 1) for i in range(1, lax.axis_size(axis) - 1)]
    return lax.ppermute(block, axis, pairs)


def pair_halo(block, axis):
    far = pair_far(block, axis)
    return pair_near(block, axis), far


def pack_kernel(send_hbm, aggregate_hbm, modes_hbm, own, message, send, aggregate, modes, sems):
    copies = [
        pltpu.make_async_copy(source, target, sems.at[i])
        for i, (source, target) in enumerate(
            ((modes_hbm, modes), (aggregate_hbm, aggregate), (send_hbm, send))
        )
    ]
    for copy in copies:
        copy.start()
    for copy in copies:
        copy.wait()
    for b in range(R):
        for m in range(MODES):
            own[b, m] = modes[m, b]
        own[b, MODES] = jnp.full((BS,), aggregate[b].astype(jnp.float32))
        own[b, MODES + 1] = jnp.zeros((BS,), jnp.float32)
    for s in range(S):
        message[s] = own[send[s]]


def plan_kernel(where, send_hbm, slab, column, live, plan, wide, raw, send, sems):
    wide_odd, narrow_odd = where[0], where[1]
    copies = [
        pltpu.make_async_copy(source, target, sems.at[i])
        for i, (source, target) in enumerate(
            ((slab, raw.at[0]), (column, raw.at[1]), (live, raw.at[2]), (send_hbm, send))
        )
    ]
    for copy in copies:
        copy.start()
    wide[...] = jnp.zeros_like(wide)
    for copy in copies:
        copy.wait()
    wide[:, :, 0:R] = raw[...]
    window, col, used = wide[0], wide[1], wide[2]
    window_row = (window * 11) >> 5
    down, across = window_row - 1, window - 3 * window_row - 1
    row_block = jnp.where(down == 0, 0, jnp.where(down == 1 - 2 * wide_odd, 1, 2))
    col_block = jnp.where(across == 0, 0, jnp.where(across == 1 - 2 * narrow_odd, 1, 2))
    block = 1 + 3 * row_block + col_block
    source = jnp.where(window == 4, col, block * S + col)
    kind = jnp.where(used == 0, 0, jnp.where((row_block == 2) & (across != 0), 2, 1))
    slot = lax.broadcasted_iota(jnp.int32, (K, BS), 0)
    lane = lax.broadcasted_iota(jnp.int32, (K, BS), 1)
    inside = lane < R
    entries = (
        (lane * K + slot)
        + (source << 8)
        + ((5 * window_row + across + 1) << 16)
        + (kind << 21)
        + (window << 23)
    )
    entries = jnp.where(inside, entries, 0)
    first = lane[0:1]
    offered = jnp.zeros((1, BS), jnp.int32)
    sent = jnp.zeros((1, BS), jnp.int32)
    for s in range(S):
        offered = jnp.where(first == send[s], 1, offered)
        sent = jnp.where(first == s, send[s], sent)
    is_live = (used != 0) & inside
    is_offered = jnp.broadcast_to(offered, (K, BS)) == 1
    before = (
        lax.broadcasted_iota(jnp.int32, (BS, BS), 0) < lax.broadcasted_iota(jnp.int32, (BS, BS), 1)
    ).astype(jnp.bfloat16)

    def counted(mask, even):
        ones = mask.astype(jnp.float32)
        ahead = [jnp.zeros((1, BS), jnp.float32)]
        for k in range(K):
            ahead.append(ahead[-1] + ones[k : k + 1])
        length = ahead.pop()
        if even:
            length = 2.0 * jnp.floor(0.5 * (length + 1.0))
        rows = jnp.broadcast_to(length, (K, BS))
        start = jnp.dot(rows.astype(jnp.bfloat16), before, preferred_element_type=jnp.float32)
        return start + jnp.concatenate(ahead, 0), jnp.sum(length, axis=1, keepdims=True)

    places, totals = [], []
    for rows in (is_offered, jnp.logical_not(is_offered)):
        top = is_live & rows & (slot == 0)
        other = is_live & rows & (slot != 0)
        place, _ = counted(top, False)
        place_other, total = counted(other, False)
        places.append((jnp.where(top, place, jnp.where(other, place_other + S, -1.0)), BS))
        totals.append(total + S)
    for i in (1, 2):
        mask = is_live & (kind == i)
        place, total = counted(mask, True)
        places.append((jnp.where(mask, place, -1.0), LIST))
        totals.append(total)
    choices = []
    for place, length in places:
        turned = place.T
        at = lax.broadcasted_iota(jnp.int32, (R, length), 1).astype(jnp.float32)
        choices.append(
            jnp.concatenate(
                [(turned[0:R, k : k + 1] == at).astype(jnp.bfloat16) for k in range(K)], 0
            )
        )
    rows = [
        jnp.concatenate([((entries >> (8 * i)) & 255)[k : k + 1, 0:R] for k in range(K)], 1)
        for i in range(4)
    ]
    rows.append(jnp.ones((1, K * R), jnp.int32))
    rows.append(jnp.zeros((11, K * R), jnp.int32))
    bytes_of = jnp.concatenate(rows, 0).astype(jnp.float32).astype(jnp.bfloat16)
    found = jnp.dot(
        bytes_of, jnp.concatenate(choices, 1), preferred_element_type=jnp.float32
    ).astype(jnp.int32)
    lists = found[0:1] + (found[1:2] << 8) + (found[2:3] << 16) + (found[3:4] << 24)
    filled = found[4:5] != 0
    plan[...] = jnp.zeros_like(plan)
    plan[0:K, 0:BS] = entries
    plan[K : K + 1, 0:BS] = sent
    numbers = jnp.where(first == 0, wide_odd, narrow_odd)
    for i, total in enumerate(totals):
        numbers = jnp.where(first == 2 + i, total.astype(jnp.int32), numbers)
    plan[K + 1 : K + 2, 0:BS] = numbers
    start = 0
    for i, ((_, length), block) in enumerate(zip(places, (0, 0, 0, 8))):
        part = slice(start, start + length)
        dummy = (25 << 16) + (block * S << 8)
        plan[LISTS + i : LISTS + i + 1, 0:length] = jnp.where(
            filled[:, part], lists[:, part], dummy
        )
        start += length


def pair_rows(high, low):
    zero = jnp.zeros_like(low)
    return jnp.concatenate(
        [jnp.concatenate([high, high], 1), jnp.concatenate([low, zero], 1)], 0
    )


def times_halves(value, halves):
    length = value.shape[0]
    both = lax.dot_general(
        pair_rows(*split(value)), halves, NT, preferred_element_type=jnp.float32
    )
    return both[:length] + both[length:]


def times_tile(value, tile):
    return times_halves(value, jnp.concatenate(split(tile), 1))


def scale_of(tile):
    eye = lax.broadcasted_iota(jnp.int32, (BS, BS), 0) == lax.broadcasted_iota(
        jnp.int32, (BS, BS), 1
    )
    diagonal = jnp.sum(jnp.where(eye, tile, 0.0), axis=0, keepdims=True)
    return jnp.broadcast_to(-OMEGA / diagonal, (GROUP, BS))


def member_marks(ints, table):
    source = (ints[0:K, 0:BS] >> 8) & 255

    def some(i, marks):
        for j in range(8):
            at = i * 8 + j
            marks = jnp.where(source == at, table[at, MODES : MODES + 1, :], marks)
        return marks

    return lax.fori_loop(0, T_ENTRIES // 8, some, jnp.zeros((K, BS), jnp.float32))


def coarse_marks(ints, members):
    return members + (((ints[0:K, 0:BS] >> 16) & 31) * AGG).astype(jnp.float32)


def fetch(tiles, entry, taken, at, sems):
    return pltpu.make_async_copy(tiles.at[entry & 255], taken.at[at], sems.at[at])


def start_batch(i, index, plan, tiles, taken, sems):
    for j in range(UNROLL):
        at = i * UNROLL + j
        pltpu.make_async_copy(
            tiles.at[plan[LISTS + index, at] & 255], taken.at[at], sems.at[i]
        ).start()


def wait_batch(i, tiles, taken, sems):
    at = pl.ds(i * UNROLL, UNROLL)
    pltpu.make_async_copy(tiles.at[pl.ds(0, UNROLL)], taken.at[at], sems.at[i]).wait()


def walk(index, plan, tiles, taken, sems, first, then):
    steps = (plan[K + 1, 2 + index] + UNROLL - 1) // UNROLL
    start_batch(0, index, plan, tiles, taken, sems)

    def start(i):
        @pl.when(i < steps)
        def _():
            start_batch(i, index, plan, tiles, taken, sems)

    start(1)
    start(2)
    wait_batch(0, tiles, taken, sems)
    first()

    def step(i, carry):
        start(i + 2)
        wait_batch(i, tiles, taken, sems)
        then(i)
        return carry

    lax.fori_loop(1, steps, step, 0)


def smooth_tiles(index, plan, tiles, table, slots, scale):
    count = plan[K + 1, 2 + index]
    for s in range(S):
        entry = plan[LISTS + index, s]
        at = entry & 255
        tile = tiles[at]
        modes = table[(entry >> 8) & 255]
        factor = scale_of(tile)
        scale[at // K] = factor
        slots[at] = times_tile(modes, tile) * factor + modes

    def some(i, carry):
        for j in range(SMOOTH):
            entry = plan[LISTS + index, jnp.minimum(S + i * SMOOTH + j, count - 1)]
            at = entry & 255
            value = times_tile(table[(entry >> 8) & 255], tiles[at])
            slots[at] = value * scale[at // K]
        return carry

    lax.fori_loop(0, (count - S + SMOOTH - 1) // SMOOTH, some, 0)


def bring_kernel(plan, tiles, halves, scale, taken, sems):
    def first():
        for s in range(S):
            tile = taken[s]
            scale[(plan[LISTS, s] & 255) // K] = scale_of(tile)
            halves[s] = jnp.concatenate(split(tile), 1)

    def then(i):
        for j in range(UNROLL):
            at = i * UNROLL + j
            halves[at] = jnp.concatenate(split(taken[at]), 1)

    walk(0, plan, tiles, taken, sems, first, then)


def offer_kernel(plan, ints, halves, scale, table, slots, message):
    count = plan[K + 1, 2]
    slots[...] = jnp.zeros_like(slots)
    marks = coarse_marks(ints, member_marks(ints, table))
    chosen = lax.broadcasted_iota(jnp.int32, (BS, BS), 0) == ints[K : K + 1, 0:BS]
    message[S * K * MODES :, :] = jnp.dot(
        marks, chosen.astype(jnp.float32), preferred_element_type=jnp.float32
    )

    def some(i, carry):
        for j in range(SMOOTH):
            place = jnp.minimum(i * SMOOTH + j, count - 1)
            entry = plan[LISTS, place]
            at = entry & 255
            modes = table[(entry >> 8) & 255]
            first = (at % K == 0).astype(jnp.float32)
            value = times_halves(modes, halves[place])
            slots[at] = value * scale[at // K] + first * modes
        return carry

    lax.fori_loop(0, (count + SMOOTH - 1) // SMOOTH, some, 0)
    for s in range(S):
        b = plan[K, s]
        for k in range(K):
            first = (s * K + k) * MODES
            message[first : first + MODES, :] = slots[b * K + k, :MODES]


def rest_kernel(
    plan, ints, tiles, table, begun, prolong_hbm, blocks, weights,
    prolong, slots, scale, marks, lab, dense_even, dense_odd, sem, sems
):
    members = member_marks(ints, table)
    coarse = coarse_marks(ints, members)
    blocks[S * K * MODES : BLOCK, :] = coarse
    blocks[BLOCK + S * K * MODES :, :] = jnp.concatenate([coarse[:, S:], coarse[:, :S]], 1)
    marks[...] = members.astype(jnp.int32) + ((ints[0:K, 0:BS] >> 23) & 15) * AGG
    copy = pltpu.make_async_copy(marks, lab, sem)
    copy.start()
    slots[...] = begun[...]
    smooth_tiles(1, plan, tiles, table, slots, scale)
    copy.wait()

    def send_row(b):
        return pltpu.make_async_copy(prolong.at[b], prolong_hbm.at[b], sems.at[b])

    def rows(i, carry):
        for j, dense in enumerate((dense_even, dense_odd)):
            b = i * 2 + j
            dense[...] = jnp.zeros_like(dense)
            for k in range(K):
                dense[lab[k, b]] += slots[b * K + k]
            for g in range(9 * AGG):
                prolong[b, MODES * g : MODES * (g + 1), :] = dense[g, :MODES]
            block, place = b // S, b % S
            start = pl.multiple_of(block * BLOCK + place * K * MODES, GROUP)
            own = jnp.concatenate([slots[b * K + k, :MODES] for k in range(K)], 0)
            blocks[pl.ds(start, K * MODES), :] = own
            high, low = split(prolong[b])
            weights[b, 0 : 9 * C, 0:BS] = high
            weights[b, 0 : 9 * C, BS:] = low
        for j in range(2):
            send_row(i * 2 + j).start()
        return carry

    lax.fori_loop(0, R // 2, rows, 0)

    def finish(b, carry):
        send_row(b).wait()
        return carry

    lax.fori_loop(0, R, finish, 0)


def couple_tiles(
    index, plan, first_block, tiles, weights, table, marks, lab, parts, products, last, totals, sem
):
    steps = jnp.maximum((plan[K + 1, 2 + index] + UNROLL - 1) // UNROLL, 2)
    for i in range(table.shape[0] // BLOCK):
        first = i * BLOCK + S * K * MODES
        marks[i * K : (i + 1) * K, :] = table[first : first + K, :].astype(jnp.int32)
    copy = pltpu.make_async_copy(marks, lab, sem)
    copy.start()
    length = K * MODES

    def apply_step(i, tiles_of=range(UNROLL)):
        for j in tiles_of:
            entry = plan[LISTS + index, i * UNROLL + j]
            source = (entry >> 8) & 255
            first = ((source >> 4) - first_block) * BLOCK + (source & 15) * length
            rows = table[pl.ds(pl.multiple_of(first, GROUP), length), :]
            high, low = split(times_tile(rows, tiles[entry & 255]))
            parts[length * j : length * (j + 1), :] = jnp.concatenate([high, low, high], 1)

    def product_step(i, products=products, tiles_of=range(UNROLL)):
        for j in tiles_of[::2]:
            b = (plan[LISTS + index, i * UNROLL + j] & 255) // K
            both = weights[b]
            at = slice(j * length, (j + 2) * length)
            products[at, :] = lax.dot_general(
                parts[at, :],
                jnp.concatenate([both[:, :BS], both], 1),
                NT,
                preferred_element_type=jnp.float32,
            )

    def place_step(i, products=products, tiles_of=range(UNROLL)):
        for j in tiles_of:
            entry = plan[LISTS + index, i * UNROLL + j]
            source = (entry >> 8) & 255
            shift = ((entry >> 16) & 31) * AGG
            major, minor = ((source >> 4) - first_block) * K, source & 15
            for g in range(K):
                at = (K * j + g) * MODES
                totals[g % 2][lab[major + g, minor] + shift] += products[at : at + GROUP, :]

    apply_step(0)
    product_step(0)
    apply_step(1)
    copy.wait()

    def step(i, carry):
        for j in range(0, UNROLL, 4):
            some = range(j, j + 4)
            place_step(i - 2, tiles_of=some)
            product_step(i - 1, tiles_of=some)
            apply_step(i, tiles_of=some)
        return carry

    lax.fori_loop(2, steps, step, 0)
    product_step(steps - 1, last)
    place_step(steps - 2)
    place_step(steps - 1, last)


def beside_kernel(
    plan, tiles, weights, table, out, marks, lab, parts, products, last, totals, sem
):
    for part in totals:
        part[0 : 25 * AGG] = jnp.zeros((25 * AGG, GROUP, 256), jnp.float32)
    couple_tiles(
        2, plan, 0, tiles, weights, table, marks, lab, parts, products, last, totals, sem
    )
    out[...] = totals[0][0 : 25 * AGG] + totals[1][0 : 25 * AGG]


def corner_kernel(
    plan, tiles, weights, begun, table, own_out, near_out, far_out,
    marks, lab, parts, products, last, totals, turned, sem
):
    totals[0][0 : 25 * AGG] = begun[...]
    totals[1][0 : 25 * AGG] = jnp.zeros((25 * AGG, GROUP, 256), jnp.float32)
    couple_tiles(
        3, plan, 8, tiles, weights, table, marks, lab, parts, products, last, totals, sem
    )
    for g in range(25 * AGG):
        turned[MODES * g : MODES * (g + 1), :] = totals[0][g, :MODES, :] + totals[1][g, :MODES, :]
    flat = turned[...].T
    even = plan[K + 1, 0] == 0
    low, mid, top = (flat[3 * C * i : 3 * C * (i + 1)] for i in range(3))
    own_out[...] = mid
    near_out[...] = jnp.where(even, top, low)
    far_out[...] = jnp.where(even, low, top)


def merge_kernel(where, own, near, far, own_out, near_out, far_out):
    even = where[0] == 0
    span = 5 * C
    low = jnp.where(even, near[...], far[...])
    top = jnp.where(even, far[...], near[...])
    zeros = jnp.zeros((3 * C, span), jnp.float32)
    mid = own[...]
    length = 5 * span
    summed = (
        jnp.concatenate([top[:, :length], zeros, zeros], 1)
        + jnp.concatenate([zeros, mid[:, :length], zeros], 1)
        + jnp.concatenate([zeros, zeros, low[:, :length]], 1)
    )
    even = where[1] == 0
    low, mid, top = (summed[C * i : C * (i + 1)] for i in range(3))
    own_out[...] = mid
    near_out[...] = jnp.where(even, top, low)
    far_out[...] = jnp.where(even, low, top)


def place_kernel(where, own, near, far, coarse):
    even = where[1] == 0
    low = jnp.where(even, near[...], far[...])
    top = jnp.where(even, far[...], near[...])
    mid = own[...]
    zeros = jnp.zeros((C, C), jnp.float32)
    pieces = []
    for u in range(7):
        lanes = slice(5 * C * u, 5 * C * (u + 1))
        pieces.append(
            jnp.concatenate([top[:, lanes], zeros, zeros], 1)
            + jnp.concatenate([zeros, mid[:, lanes], zeros], 1)
            + jnp.concatenate([zeros, zeros, low[:, lanes]], 1)
        )
    coarse[...] = jnp.concatenate(pieces, 1)


def shape(*dims, dtype=jnp.float32):
    return jax.ShapeDtypeStruct(dims, dtype)


def body(operator_tiles, tile_slab, tile_column, tile_live, send_list, aggregate, null_modes):
    tiles = operator_tiles[0, 0]
    slab = tile_slab[0, 0].T
    column = tile_column[0, 0].T
    live = tile_live[0, 0].T
    send = send_list[0, 0]
    wide_odd = lax.axis_index("wide") % 2
    narrow_odd = lax.axis_index("narrow") % 2
    where = jnp.stack([wide_odd, narrow_odd]).astype(jnp.int32)

    own_modes, offered = pl.pallas_call(
        pack_kernel,
        out_shape=(shape(R, GROUP, BS), shape(S, GROUP, BS)),
        in_specs=[HBM] * 3,
        out_specs=(VMEM, VMEM),
        scratch_shapes=[
            pltpu.SMEM((S,), jnp.int32),
            pltpu.SMEM((R,), jnp.int32),
            pltpu.VMEM((MODES, R, BS), jnp.float32),
            pltpu.SemaphoreType.DMA((3,)),
        ],
        compiler_params=params(4),
        name="pack",
    )(
        *(
            pltpu.with_memory_space_constraint(x, pltpu.HBM)
            for x in (send, aggregate[0, 0], null_modes[0, 0].transpose(1, 0, 2))
        )
    )
    near, far = pair_halo(offered, "narrow")
    plan = pl.pallas_call(
        plan_kernel,
        out_shape=shape(16, LIST, dtype=jnp.int32),
        in_specs=[SMEM] + [HBM] * 4,
        out_specs=VMEM,
        scratch_shapes=[
            pltpu.VMEM((3, K, BS), jnp.int32),
            pltpu.VMEM((3, K, R), jnp.int32),
            pltpu.SMEM((S,), jnp.int32),
            pltpu.SemaphoreType.DMA((4,)),
        ],
        compiler_params=params(8),
        cost_estimate=pl.CostEstimate(flops=10**8, bytes_accessed=5 * 10**6, transcendentals=0),
        name="plan",
    )(where, *(pltpu.with_memory_space_constraint(x, pltpu.HBM) for x in (send, slab, column, live)))
    line = jnp.concatenate([offered, near, far], 0)
    line, plan = lax.optimization_barrier((line, plan))
    wide_near, wide_far = pair_halo(line, "wide")
    table = jnp.concatenate([own_modes, near, far, wide_near, wide_far], 0)

    tiles = tiles.reshape(R * K, BS, BS)
    resting = pltpu.with_memory_space_constraint(tiles, pltpu.HBM)
    taken = pltpu.VMEM((S * K, BS, BS), jnp.float32)
    scales = pltpu.VMEM((R, GROUP, BS), jnp.float32)
    halves, offered_scale = pl.pallas_call(
        bring_kernel,
        out_shape=(shape(S * K, BS, 2 * BS, dtype=jnp.bfloat16), shape(R, GROUP, BS)),
        in_specs=[SMEM, HBM],
        out_specs=(VMEM, VMEM),
        scratch_shapes=[taken, pltpu.SemaphoreType.DMA((S * K // UNROLL,))],
        compiler_params=params(24),
        cost_estimate=pl.CostEstimate(flops=10**8, bytes_accessed=10**7, transcendentals=0),
        name="bring",
    )(plan, resting)
    begun, message = pl.pallas_call(
        offer_kernel,
        out_shape=(shape(R * K, GROUP, BS), shape(BLOCK, BS)),
        in_specs=[SMEM, VMEM, VMEM, VMEM, VMEM],
        out_specs=(VMEM, VMEM),
        compiler_params=params(16),
        cost_estimate=pl.CostEstimate(flops=10**8, bytes_accessed=4 * 10**7, transcendentals=0),
        name="offer",
    )(plan, plan, halves, offered_scale, table)

    narrow_near, narrow_far = pair_halo(message, "narrow")
    wide_own = pair_far(message, "wide")
    prolong, blocks, weights = pl.pallas_call(
        rest_kernel,
        out_shape=(
            shape(R, 9 * C, BS),
            shape(2 * BLOCK, BS),
            shape(R, 256, 2 * BS, dtype=jnp.bfloat16),
        ),
        in_specs=[SMEM, VMEM, VMEM, VMEM, VMEM],
        out_specs=(HBM, VMEM, VMEM),
        scratch_shapes=[
            pltpu.VMEM((R, 9 * C, BS), jnp.float32),
            pltpu.VMEM((R * K, GROUP, BS), jnp.float32),
            scales,
            pltpu.VMEM((K, BS), jnp.int32),
            pltpu.SMEM((K, BS), jnp.int32),
            pltpu.VMEM((9 * AGG, GROUP, BS), jnp.float32),
            pltpu.VMEM((9 * AGG, GROUP, BS), jnp.float32),
            pltpu.SemaphoreType.DMA,
            pltpu.SemaphoreType.DMA((R,)),
        ],
        compiler_params=params(24),
        cost_estimate=pl.CostEstimate(flops=2 * 10**9, bytes_accessed=2 * 10**7, transcendentals=0),
        name="rest",
    )(plan, plan, tiles, table, begun)
    sides = jnp.concatenate([narrow_near, narrow_far], 0)
    line = jnp.concatenate([message, narrow_near, narrow_far], 0)
    line, sides, weights, wide_own = lax.optimization_barrier((line, sides, weights, wide_own))
    wide_near = pair_near(line, "wide")
    wide_far = pair_far(sides, "wide")

    def coupling(blocks):
        return [
            pltpu.VMEM((blocks * K, BS), jnp.int32),
            pltpu.SMEM((blocks * K, BS), jnp.int32),
            pltpu.VMEM((UNROLL * K * MODES, 3 * BS), jnp.bfloat16),
            pltpu.VMEM((UNROLL * K * MODES + GROUP, 256), jnp.float32),
            pltpu.VMEM((UNROLL * K * MODES + GROUP, 256), jnp.float32),
            [pltpu.VMEM((25 * AGG + 52, GROUP, 256), jnp.float32)] * 2,
        ]

    table = jnp.concatenate([blocks, narrow_near, narrow_far, wide_near, wide_own], 0)
    total = pl.pallas_call(
        beside_kernel,
        out_shape=shape(25 * AGG, GROUP, 256),
        in_specs=[SMEM] + [VMEM] * 3,
        out_specs=VMEM,
        scratch_shapes=coupling(8) + [pltpu.SemaphoreType.DMA],
        compiler_params=params(16),
        cost_estimate=pl.CostEstimate(flops=8 * 10**9, bytes_accessed=3 * 10**7, transcendentals=0),
        name="beside",
    )(plan, tiles, weights, table)
    own, near, far = pl.pallas_call(
        corner_kernel,
        out_shape=(shape(3 * C, 25 * C),) * 3,
        in_specs=[SMEM] + [VMEM] * 4,
        out_specs=(VMEM,) * 3,
        scratch_shapes=coupling(2)
        + [pltpu.VMEM((25 * C, 256), jnp.float32), pltpu.SemaphoreType.DMA],
        compiler_params=params(16),
        name="corner",
    )(plan, tiles, weights, total, wide_far)

    size = lax.axis_size("wide")
    pairs = [(i, i ^ 1) for i in range(size)]
    far_pairs = [(i, i + 1) if i % 2 else (i, i - 1) for i in range(1, size - 1)]
    near, far = lax.ppermute(near, "wide", pairs), lax.ppermute(far, "wide", far_pairs)
    own, near, far = pl.pallas_call(
        merge_kernel,
        out_shape=(shape(C, 35 * C),) * 3,
        in_specs=[SMEM] + [VMEM] * 3,
        out_specs=(VMEM,) * 3,
        compiler_params=params(4),
        name="merge",
    )(where, own, near, far)
    size = lax.axis_size("narrow")
    pairs = [(i, i ^ 1) for i in range(size)]
    far_pairs = [(i, i + 1) if i % 2 else (i, i - 1) for i in range(1, size - 1)]
    near, far = lax.ppermute(near, "narrow", pairs), lax.ppermute(far, "narrow", far_pairs)
    coarse = pl.pallas_call(
        place_kernel,
        out_shape=shape(C, 49 * C),
        in_specs=[SMEM] + [VMEM] * 3,
        out_specs=VMEM,
        compiler_params=params(4),
        name="place",
    )(where, own, near, far)
    return prolong[None, None], coarse[None, None]


def solution(mesh):
    in_specs = (
        P("wide", "narrow", None, None, None, None),
        P("wide", "narrow", None, None),
        P("wide", "narrow", None, None),
        P("wide", "narrow", None, None),
        P("wide", "narrow", None),
        P("wide", "narrow", None),
        P("wide", "narrow", None, None, None),
    )
    out_specs = (P("wide", "narrow", None, None, None), P("wide", "narrow", None, None))
    return jax.shard_map(body, mesh=mesh, in_specs=in_specs, out_specs=out_specs, check_vma=False)
```

```python
import functools

import jax
import jax.numpy as jnp
from jax import lax
from jax.experimental import pallas as pl
from jax.experimental.pallas import tpu as pltpu
from jax.sharding import PartitionSpec as P

MODES = 6
GROUP = 8
AGG = 4
BS = 128
R = 32
K = 8
S = 16
C = 24
OMEGA = 0.7
BLOCK = S * K * MODES + GROUP
T_ENTRIES = R + 8 * S
UNROLL = 16
ROWS = 4
SMOOTH = 32
LIST = 384
LISTS = K + 2
NT = (((1,), (1,)), ((), ()))
VMEM = pl.BlockSpec(memory_space=pltpu.VMEM)
SMEM = pl.BlockSpec(memory_space=pltpu.SMEM)
HBM = pl.BlockSpec(memory_space=pltpu.HBM)


def params(mib):
    return pltpu.CompilerParams(vmem_limit_bytes=mib * 2**20)


def split(value):
    high = value.astype(jnp.bfloat16)
    return high, (value - high.astype(jnp.float32)).astype(jnp.bfloat16)


def pair_near(block, axis):
    return lax.ppermute(block, axis, [(i, i ^ 1) for i in range(lax.axis_size(axis))])


def pair_far(block, axis):
    pairs = [(i, i + 1) if i % 2 else (i, i - 1) for i in range(1, lax.axis_size(axis) - 1)]
    return lax.ppermute(block, axis, pairs)


def pair_halo(block, axis):
    far = pair_far(block, axis)
    return pair_near(block, axis), far


def pack_kernel(send_hbm, aggregate_hbm, modes_hbm, own, message, send, aggregate, modes, sems):
    copies = [
        pltpu.make_async_copy(source, target, sems.at[i])
        for i, (source, target) in enumerate(
            ((modes_hbm, modes), (aggregate_hbm, aggregate), (send_hbm, send))
        )
    ]
    for copy in copies:
        copy.start()
    for copy in copies:
        copy.wait()
    for b in range(R):
        for m in range(MODES):
            own[b, m] = modes[m, b]
        own[b, MODES] = jnp.full((BS,), aggregate[b].astype(jnp.float32))
        own[b, MODES + 1] = jnp.zeros((BS,), jnp.float32)
    for s in range(S):
        message[s] = own[send[s]]


def plan_kernel(where, send_hbm, slab, column, live, plan, wide, raw, send, sems):
    wide_odd, narrow_odd = where[0], where[1]
    copies = [
        pltpu.make_async_copy(source, target, sems.at[i])
        for i, (source, target) in enumerate(
            ((slab, raw.at[0]), (column, raw.at[1]), (live, raw.at[2]), (send_hbm, send))
        )
    ]
    for copy in copies:
        copy.start()
    wide[...] = jnp.zeros_like(wide)
    for copy in copies:
        copy.wait()
    wide[:, :, 0:R] = raw[...]
    window, col, used = wide[0], wide[1], wide[2]
    window_row = (window * 11) >> 5
    down, across = window_row - 1, window - 3 * window_row - 1
    is_near, is_far = down == 1 - 2 * wide_odd, down == 2 * wide_odd - 1
    side = jnp.where(across == 0, 2, jnp.where(across == 1 - 2 * narrow_odd, 1, 0))
    block = side + jnp.where(is_near, 7, jnp.where(is_far, 4, 2))
    source = jnp.where(window == 4, col, block * S + col)
    kind = jnp.where(used == 0, 0, jnp.where(is_far & (across != 0), 2, 1))
    slot = lax.broadcasted_iota(jnp.int32, (K, BS), 0)
    lane = lax.broadcasted_iota(jnp.int32, (K, BS), 1)
    inside = lane < R
    entries = (
        (lane * K + slot)
        + (source << 8)
        + ((5 * window_row + across + 1) << 16)
        + (kind << 21)
        + (window << 23)
    )
    entries = jnp.where(inside, entries, 0)
    first = lane[0:1]
    offered = jnp.zeros((1, BS), jnp.int32)
    sent = jnp.zeros((1, BS), jnp.int32)
    for s in range(S):
        offered = jnp.where(first == send[s], 1, offered)
        sent = jnp.where(first == s, send[s], sent)
    is_live = (used != 0) & inside
    is_offered = jnp.broadcast_to(offered, (K, BS)) == 1
    before = (
        lax.broadcasted_iota(jnp.int32, (BS, BS), 0) < lax.broadcasted_iota(jnp.int32, (BS, BS), 1)
    ).astype(jnp.bfloat16)

    def counted(mask, even):
        ones = mask.astype(jnp.float32)
        ahead = [jnp.zeros((1, BS), jnp.float32)]
        for k in range(K):
            ahead.append(ahead[-1] + ones[k : k + 1])
        length = ahead.pop()
        if even:
            length = 2.0 * jnp.floor(0.5 * (length + 1.0))
        rows = jnp.broadcast_to(length, (K, BS))
        start = jnp.dot(rows.astype(jnp.bfloat16), before, preferred_element_type=jnp.float32)
        return start + jnp.concatenate(ahead, 0), jnp.sum(length, axis=1, keepdims=True)

    places, totals = [], []
    for rows in (is_offered, jnp.logical_not(is_offered)):
        top = is_live & rows & (slot == 0)
        other = is_live & rows & (slot != 0)
        place, _ = counted(top, False)
        place_other, total = counted(other, False)
        places.append((jnp.where(top, place, jnp.where(other, place_other + S, -1.0)), BS))
        totals.append(total + S)
    for i in (1, 2):
        mask = is_live & (kind == i)
        place, total = counted(mask, True)
        places.append((jnp.where(mask, place, -1.0), LIST))
        totals.append(total)
    choices = []
    for place, length in places:
        turned = place.T
        at = lax.broadcasted_iota(jnp.int32, (R, length), 1).astype(jnp.float32)
        choices.append(
            jnp.concatenate(
                [(turned[0:R, k : k + 1] == at).astype(jnp.bfloat16) for k in range(K)], 0
            )
        )
    rows = [
        jnp.concatenate([((entries >> (8 * i)) & 255)[k : k + 1, 0:R] for k in range(K)], 1)
        for i in range(4)
    ]
    rows.append(jnp.ones((1, K * R), jnp.int32))
    rows.append(jnp.zeros((11, K * R), jnp.int32))
    bytes_of = jnp.concatenate(rows, 0).astype(jnp.float32).astype(jnp.bfloat16)
    found = jnp.dot(
        bytes_of, jnp.concatenate(choices, 1), preferred_element_type=jnp.float32
    ).astype(jnp.int32)
    lists = found[0:1] + (found[1:2] << 8) + (found[2:3] << 16) + (found[3:4] << 24)
    filled = found[4:5] != 0
    plan[...] = jnp.zeros_like(plan)
    plan[0:K, 0:BS] = entries
    plan[K : K + 1, 0:BS] = sent
    numbers = jnp.where(first == 0, wide_odd, narrow_odd)
    for i, total in enumerate(totals):
        numbers = jnp.where(first == 2 + i, total.astype(jnp.int32), numbers)
    plan[K + 1 : K + 2, 0:BS] = numbers
    start = 0
    for i, ((_, length), block) in enumerate(zip(places, (0, 0, 0, 4))):
        part = slice(start, start + length)
        dummy = (25 << 16) + (block * S << 8)
        plan[LISTS + i : LISTS + i + 1, 0:length] = jnp.where(
            filled[:, part], lists[:, part], dummy
        )
        start += length


def pair_rows(high, low):
    zero = jnp.zeros_like(low)
    return jnp.concatenate(
        [jnp.concatenate([high, high], 1), jnp.concatenate([low, zero], 1)], 0
    )


def times_halves(value, halves):
    length = value.shape[0]
    both = lax.dot_general(
        pair_rows(*split(value)), halves, NT, preferred_element_type=jnp.float32
    )
    return both[:length] + both[length:]


def times_tile(value, tile):
    return times_halves(value, jnp.concatenate(split(tile), 1))


def scale_of(tile):
    eye = lax.broadcasted_iota(jnp.int32, (BS, BS), 0) == lax.broadcasted_iota(
        jnp.int32, (BS, BS), 1
    )
    diagonal = jnp.sum(jnp.where(eye, tile, 0.0), axis=0, keepdims=True)
    return jnp.broadcast_to(-OMEGA / diagonal, (GROUP, BS))


def member_marks(ints, table):
    source = (ints[0:K, 0:BS] >> 8) & 255

    def some(i, marks):
        for j in range(8):
            at = i * 8 + j
            marks = jnp.where(source == at, table[at, MODES : MODES + 1, :], marks)
        return marks

    return lax.fori_loop(0, T_ENTRIES // 8, some, jnp.zeros((K, BS), jnp.float32))


def coarse_marks(ints, members):
    return members + (((ints[0:K, 0:BS] >> 16) & 31) * AGG).astype(jnp.float32)


def fetch(tiles, entry, taken, at, sems):
    return pltpu.make_async_copy(tiles.at[entry & 255], taken.at[at], sems.at[at])


def start_batch(i, index, plan, tiles, taken, sems):
    for j in range(UNROLL):
        at = i * UNROLL + j
        pltpu.make_async_copy(
            tiles.at[plan[LISTS + index, at] & 255], taken.at[at], sems.at[i]
        ).start()


def wait_batch(i, tiles, taken, sems):
    at = pl.ds(i * UNROLL, UNROLL)
    pltpu.make_async_copy(tiles.at[pl.ds(0, UNROLL)], taken.at[at], sems.at[i]).wait()


def walk(index, plan, tiles, taken, sems, first, then):
    steps = (plan[K + 1, 2 + index] + UNROLL - 1) // UNROLL
    start_batch(0, index, plan, tiles, taken, sems)

    def start(i):
        @pl.when(i < steps)
        def _():
            start_batch(i, index, plan, tiles, taken, sems)

    start(1)
    start(2)
    wait_batch(0, tiles, taken, sems)
    first()
    for i in range(1, S * K // UNROLL):

        @pl.when(i < steps)
        def _(i=i):
            if i + 2 < S * K // UNROLL:
                start(i + 2)
            wait_batch(i, tiles, taken, sems)
            then(i)


def smooth_tiles(index, plan, tiles, table, slots, scale):
    count = plan[K + 1, 2 + index]
    for s in range(S):
        entry = plan[LISTS + index, s]
        at = entry & 255
        tile = tiles[at]
        modes = table[(entry >> 8) & 255]
        factor = scale_of(tile)
        scale[at // K] = factor
        slots[at] = times_tile(modes, tile) * factor + modes

    def some(i, carry):
        for j in range(SMOOTH):
            entry = plan[LISTS + index, jnp.minimum(S + i * SMOOTH + j, count - 1)]
            at = entry & 255
            value = times_tile(table[(entry >> 8) & 255], tiles[at])
            slots[at] = value * scale[at // K]
        return carry

    lax.fori_loop(0, (count - S + SMOOTH - 1) // SMOOTH, some, 0)


def bring_kernel(plan, tiles, halves, scale, taken, sems):
    def first():
        for s in range(S):
            tile = taken[s]
            scale[(plan[LISTS, s] & 255) // K] = scale_of(tile)
            halves[s] = jnp.concatenate(split(tile), 1)

    def then(i):
        for j in range(UNROLL):
            at = i * UNROLL + j
            halves[at] = jnp.concatenate(split(taken[at]), 1)

    walk(0, plan, tiles, taken, sems, first, then)


def offer_kernel(plan, ints, halves, scale, table, slots, message):
    count = plan[K + 1, 2]
    slots[...] = jnp.zeros_like(slots)
    marks = coarse_marks(ints, member_marks(ints, table))
    chosen = lax.broadcasted_iota(jnp.int32, (BS, BS), 0) == ints[K : K + 1, 0:BS]
    message[S * K * MODES :, :] = jnp.dot(
        marks, chosen.astype(jnp.float32), preferred_element_type=jnp.float32
    )

    def some(i, carry):
        for j in range(SMOOTH):
            place = jnp.minimum(i * SMOOTH + j, count - 1)
            entry = plan[LISTS, place]
            at = entry & 255
            modes = table[(entry >> 8) & 255]
            first = (at % K == 0).astype(jnp.float32)
            value = times_halves(modes, halves[place])
            slots[at] = value * scale[at // K] + first * modes
        return carry

    lax.fori_loop(0, (count + SMOOTH - 1) // SMOOTH, some, 0)
    for s in range(S):
        b = plan[K, s]
        for k in range(K):
            first = (s * K + k) * MODES
            message[first : first + MODES, :] = slots[b * K + k, :MODES]


def rest_kernel(
    plan, ints, tiles, table, begun, prolong_hbm, blocks, weights,
    prolong, slots, scale, marks, lab, dense_refs, sem, sems
):
    members = member_marks(ints, table)
    coarse = coarse_marks(ints, members)
    blocks[S * K * MODES : BLOCK, :] = coarse
    blocks[BLOCK + S * K * MODES :, :] = jnp.concatenate([coarse[:, S:], coarse[:, :S]], 1)
    marks[...] = members.astype(jnp.int32) + ((ints[0:K, 0:BS] >> 23) & 15) * AGG
    copy = pltpu.make_async_copy(marks, lab, sem)
    copy.start()
    slots[...] = begun[...]
    smooth_tiles(1, plan, tiles, table, slots, scale)
    copy.wait()

    def send_row(b):
        return pltpu.make_async_copy(prolong.at[b], prolong_hbm.at[b], sems.at[b])

    def rows(i, carry):
        for j, dense in enumerate(dense_refs):
            b = i * ROWS + j
            dense[...] = jnp.zeros_like(dense)
            for k in range(K):
                dense[lab[k, b]] += slots[b * K + k]
            for g in range(9 * AGG):
                prolong[b, MODES * g : MODES * (g + 1), :] = dense[g, :MODES]
            block, place = b // S, b % S
            start = pl.multiple_of(block * BLOCK + place * K * MODES, GROUP)
            own = jnp.concatenate([slots[b * K + k, :MODES] for k in range(K)], 0)
            blocks[pl.ds(start, K * MODES), :] = own
            high, low = split(prolong[b])
            weights[b, 0 : 9 * C, 0:BS] = high
            weights[b, 0 : 9 * C, BS:] = low
        for j in range(ROWS):
            send_row(i * ROWS + j).start()
        return carry

    lax.fori_loop(0, R // ROWS, rows, 0)

    def finish(b, carry):
        send_row(b).wait()
        return carry

    lax.fori_loop(0, R, finish, 0)


def couple_tiles(
    index, plan, first_block, tiles, weights, table, marks, lab, parts, products, last, totals, sem
):
    steps = jnp.maximum((plan[K + 1, 2 + index] + UNROLL - 1) // UNROLL, 2)
    for i in range(table.shape[0] // BLOCK):
        first = i * BLOCK + S * K * MODES
        marks[i * K : (i + 1) * K, :] = table[first : first + K, :].astype(jnp.int32)
    copy = pltpu.make_async_copy(marks, lab, sem)
    copy.start()
    length = K * MODES

    def apply_step(i, tiles_of=range(UNROLL)):
        for j in tiles_of:
            entry = plan[LISTS + index, i * UNROLL + j]
            source = (entry >> 8) & 255
            first = ((source >> 4) - first_block) * BLOCK + (source & 15) * length
            rows = table[pl.ds(pl.multiple_of(first, GROUP), length), :]
            high, low = split(times_tile(rows, tiles[entry & 255]))
            parts[length * j : length * (j + 1), :] = jnp.concatenate([high, low, high], 1)

    def product_step(i, products=products, tiles_of=range(UNROLL)):
        for j in tiles_of[::2]:
            b = (plan[LISTS + index, i * UNROLL + j] & 255) // K
            both = weights[b]
            at = slice(j * length, (j + 2) * length)
            products[at, :] = lax.dot_general(
                parts[at, :],
                jnp.concatenate([both[:, :BS], both], 1),
                NT,
                preferred_element_type=jnp.float32,
            )

    def place_step(i, products=products, tiles_of=range(UNROLL)):
        for j in tiles_of:
            entry = plan[LISTS + index, i * UNROLL + j]
            source = (entry >> 8) & 255
            shift = ((entry >> 16) & 31) * AGG
            major, minor = ((source >> 4) - first_block) * K, source & 15
            for g in range(K):
                at = (K * j + g) * MODES
                totals[g % 2][lab[major + g, minor] + shift] += products[at : at + GROUP, :]

    apply_step(0)
    product_step(0)
    apply_step(1)
    copy.wait()

    def step(i, carry):
        for j in range(0, UNROLL, 4):
            some = range(j, j + 4)
            place_step(i - 2, tiles_of=some)
            product_step(i - 1, tiles_of=some)
            apply_step(i, tiles_of=some)
        return carry

    lax.fori_loop(2, steps, step, 0)
    product_step(steps - 1, last)
    place_step(steps - 2)
    place_step(steps - 1, last)


def beside_kernel(
    plan, tiles, weights, table, out, marks, lab, parts, products, last, totals, sem
):
    for part in totals:
        part[0 : 25 * AGG] = jnp.zeros((25 * AGG, GROUP, 256), jnp.float32)
    couple_tiles(
        2, plan, 0, tiles, weights, table, marks, lab, parts, products, last, totals, sem
    )
    out[...] = totals[0][0 : 25 * AGG] + totals[1][0 : 25 * AGG]


def corner_kernel(
    plan, tiles, weights, begun, table, own_out, near_out, far_out,
    marks, lab, parts, products, last, totals, turned, sem
):
    totals[0][0 : 25 * AGG] = begun[...]
    totals[1][0 : 25 * AGG] = jnp.zeros((25 * AGG, GROUP, 256), jnp.float32)
    couple_tiles(
        3, plan, 4, tiles, weights, table, marks, lab, parts, products, last, totals, sem
    )
    for g in range(25 * AGG):
        turned[MODES * g : MODES * (g + 1), :] = totals[0][g, :MODES, :] + totals[1][g, :MODES, :]
    flat = turned[...].T
    even = plan[K + 1, 0] == 0
    low, mid, top = (flat[3 * C * i : 3 * C * (i + 1)] for i in range(3))
    own_out[...] = mid
    near_out[...] = jnp.where(even, top, low)
    far_out[...] = jnp.where(even, low, top)


def merge_kernel(where, blocks, own_out, near_out, far_out):
    even = where[0] == 0
    span = 5 * C
    mid, near, far = (blocks[3 * C * i : 3 * C * (i + 1), :] for i in range(3))
    low = jnp.where(even, near, far)
    top = jnp.where(even, far, near)
    zeros = jnp.zeros((3 * C, span), jnp.float32)
    length = 5 * span
    summed = (
        jnp.concatenate([top[:, :length], zeros, zeros], 1)
        + jnp.concatenate([zeros, mid[:, :length], zeros], 1)
        + jnp.concatenate([zeros, zeros, low[:, :length]], 1)
    )
    even = where[1] == 0
    low, mid, top = (summed[C * i : C * (i + 1)] for i in range(3))
    own_out[...] = mid
    near_out[...] = jnp.where(even, top, low)
    far_out[...] = jnp.where(even, low, top)


def place_kernel(where, own, near, far, coarse):
    even = where[1] == 0
    low = jnp.where(even, near[...], far[...])
    top = jnp.where(even, far[...], near[...])
    mid = own[...]
    zeros = jnp.zeros((C, C), jnp.float32)
    pieces = []
    for u in range(7):
        lanes = slice(5 * C * u, 5 * C * (u + 1))
        pieces.append(
            jnp.concatenate([top[:, lanes], zeros, zeros], 1)
            + jnp.concatenate([zeros, mid[:, lanes], zeros], 1)
            + jnp.concatenate([zeros, zeros, low[:, lanes]], 1)
        )
    coarse[...] = jnp.concatenate(pieces, 1)


def shape(*dims, dtype=jnp.float32):
    return jax.ShapeDtypeStruct(dims, dtype)


def body(operator_tiles, tile_slab, tile_column, tile_live, send_list, aggregate, null_modes):
    tiles = operator_tiles[0, 0]
    slab = tile_slab[0, 0].T
    column = tile_column[0, 0].T
    live = tile_live[0, 0].T
    send = send_list[0, 0]
    wide_odd = lax.axis_index("wide") % 2
    narrow_odd = lax.axis_index("narrow") % 2
    where = jnp.stack([wide_odd, narrow_odd]).astype(jnp.int32)

    own_modes, offered = pl.pallas_call(
        pack_kernel,
        out_shape=(shape(R, GROUP, BS), shape(S, GROUP, BS)),
        in_specs=[HBM] * 3,
        out_specs=(VMEM, VMEM),
        scratch_shapes=[
            pltpu.SMEM((S,), jnp.int32),
            pltpu.SMEM((R,), jnp.int32),
            pltpu.VMEM((MODES, R, BS), jnp.float32),
            pltpu.SemaphoreType.DMA((3,)),
        ],
        compiler_params=params(4),
        name="pack",
    )(
        *(
            pltpu.with_memory_space_constraint(x, pltpu.HBM)
            for x in (send, aggregate[0, 0], null_modes[0, 0].transpose(1, 0, 2))
        )
    )
    near, far = pair_halo(offered, "narrow")
    plan = pl.pallas_call(
        plan_kernel,
        out_shape=shape(16, LIST, dtype=jnp.int32),
        in_specs=[SMEM] + [HBM] * 4,
        out_specs=VMEM,
        scratch_shapes=[
            pltpu.VMEM((3, K, BS), jnp.int32),
            pltpu.VMEM((3, K, R), jnp.int32),
            pltpu.SMEM((S,), jnp.int32),
            pltpu.SemaphoreType.DMA((4,)),
        ],
        compiler_params=params(8),
        cost_estimate=pl.CostEstimate(flops=10**8, bytes_accessed=5 * 10**6, transcendentals=0),
        name="plan",
    )(where, *(pltpu.with_memory_space_constraint(x, pltpu.HBM) for x in (send, slab, column, live)))
    line = jnp.concatenate([far, near, offered], 0)
    line, plan = lax.optimization_barrier((line, plan))
    wide_near, wide_far = pair_halo(line, "wide")
    table = jnp.concatenate([own_modes, far, near, wide_far, wide_near], 0)

    tiles = tiles.reshape(R * K, BS, BS)
    resting = pltpu.with_memory_space_constraint(tiles, pltpu.HBM)
    taken = pltpu.VMEM((S * K, BS, BS), jnp.float32)
    scales = pltpu.VMEM((R, GROUP, BS), jnp.float32)
    halves, offered_scale = pl.pallas_call(
        bring_kernel,
        out_shape=(shape(S * K, BS, 2 * BS, dtype=jnp.bfloat16), shape(R, GROUP, BS)),
        in_specs=[SMEM, HBM],
        out_specs=(VMEM, VMEM),
        scratch_shapes=[taken, pltpu.SemaphoreType.DMA((S * K // UNROLL,))],
        compiler_params=params(24),
        cost_estimate=pl.CostEstimate(flops=10**8, bytes_accessed=10**7, transcendentals=0),
        name="bring",
    )(plan, resting)
    begun, message = pl.pallas_call(
        offer_kernel,
        out_shape=(shape(R * K, GROUP, BS), shape(BLOCK, BS)),
        in_specs=[SMEM, VMEM, VMEM, VMEM, VMEM],
        out_specs=(VMEM, VMEM),
        compiler_params=params(16),
        cost_estimate=pl.CostEstimate(flops=10**8, bytes_accessed=4 * 10**7, transcendentals=0),
        name="offer",
    )(plan, plan, halves, offered_scale, table)

    narrow_near, narrow_far = pair_halo(message, "narrow")
    wide_own = pair_far(message, "wide")
    prolong, blocks, weights = pl.pallas_call(
        rest_kernel,
        out_shape=(
            shape(R, 9 * C, BS),
            shape(2 * BLOCK, BS),
            shape(R, 256, 2 * BS, dtype=jnp.bfloat16),
        ),
        in_specs=[SMEM, VMEM, VMEM, VMEM, VMEM],
        out_specs=(HBM, VMEM, VMEM),
        scratch_shapes=[
            pltpu.VMEM((R, 9 * C, BS), jnp.float32),
            pltpu.VMEM((R * K, GROUP, BS), jnp.float32),
            scales,
            pltpu.VMEM((K, BS), jnp.int32),
            pltpu.SMEM((K, BS), jnp.int32),
            [pltpu.VMEM((9 * AGG, GROUP, BS), jnp.float32)] * ROWS,
            pltpu.SemaphoreType.DMA,
            pltpu.SemaphoreType.DMA((R,)),
        ],
        compiler_params=params(24),
        cost_estimate=pl.CostEstimate(flops=2 * 10**9, bytes_accessed=2 * 10**7, transcendentals=0),
        name="rest",
    )(plan, plan, tiles, table, begun)
    sides = jnp.concatenate([narrow_far, narrow_near], 0)
    line = jnp.concatenate([narrow_far, narrow_near, message], 0)
    line, sides, weights, wide_own = lax.optimization_barrier((line, sides, weights, wide_own))
    wide_near = pair_near(line, "wide")
    wide_far = pair_far(sides, "wide")

    def coupling(blocks):
        return [
            pltpu.VMEM((blocks * K, BS), jnp.int32),
            pltpu.SMEM((blocks * K, BS), jnp.int32),
            pltpu.VMEM((UNROLL * K * MODES, 3 * BS), jnp.bfloat16),
            pltpu.VMEM((UNROLL * K * MODES + GROUP, 256), jnp.float32),
            pltpu.VMEM((UNROLL * K * MODES + GROUP, 256), jnp.float32),
            [pltpu.VMEM((25 * AGG + 52, GROUP, 256), jnp.float32)] * 2,
        ]

    table = jnp.concatenate([blocks, sides, sides, wide_own, wide_near], 0)
    total = pl.pallas_call(
        beside_kernel,
        out_shape=shape(25 * AGG, GROUP, 256),
        in_specs=[SMEM] + [VMEM] * 3,
        out_specs=VMEM,
        scratch_shapes=coupling(10) + [pltpu.SemaphoreType.DMA],
        compiler_params=params(16),
        cost_estimate=pl.CostEstimate(flops=8 * 10**9, bytes_accessed=3 * 10**7, transcendentals=0),
        name="beside",
    )(plan, tiles, weights, table)
    own, near, far = pl.pallas_call(
        corner_kernel,
        out_shape=(shape(3 * C, 25 * C),) * 3,
        in_specs=[SMEM] + [VMEM] * 4,
        out_specs=(VMEM,) * 3,
        scratch_shapes=coupling(2)
        + [pltpu.VMEM((25 * C, 256), jnp.float32), pltpu.SemaphoreType.DMA],
        compiler_params=params(16),
        name="corner",
    )(plan, tiles, weights, total, wide_far)

    size = lax.axis_size("wide")
    pairs = [(i, i ^ 1) for i in range(size)]
    far_pairs = [(i, i + 1) if i % 2 else (i, i - 1) for i in range(1, size - 1)]
    near, far = lax.ppermute(near, "wide", pairs), lax.ppermute(far, "wide", far_pairs)
    own, near, far = pl.pallas_call(
        merge_kernel,
        out_shape=(shape(C, 35 * C),) * 3,
        in_specs=[SMEM, VMEM],
        out_specs=(VMEM,) * 3,
        compiler_params=params(4),
        name="merge",
    )(where, jnp.concatenate([own, near, far], 0))
    size = lax.axis_size("narrow")
    pairs = [(i, i ^ 1) for i in range(size)]
    far_pairs = [(i, i + 1) if i % 2 else (i, i - 1) for i in range(1, size - 1)]
    near, far = lax.ppermute(near, "narrow", pairs), lax.ppermute(far, "narrow", far_pairs)
    coarse = pl.pallas_call(
        place_kernel,
        out_shape=shape(C, 49 * C),
        in_specs=[SMEM] + [VMEM] * 3,
        out_specs=VMEM,
        compiler_params=params(4),
        name="place",
    )(where, own, near, far)
    return prolong[None, None], coarse[None, None]


def solution(mesh):
    in_specs = (
        P("wide", "narrow", None, None, None, None),
        P("wide", "narrow", None, None),
        P("wide", "narrow", None, None),
        P("wide", "narrow", None, None),
        P("wide", "narrow", None),
        P("wide", "narrow", None),
        P("wide", "narrow", None, None, None),
    )
    out_specs = (P("wide", "narrow", None, None, None), P("wide", "narrow", None, None))
    return jax.shard_map(body, mesh=mesh, in_specs=in_specs, out_specs=out_specs, check_vma=False)
```

```python
import functools

import jax
import jax.numpy as jnp
from jax import lax
from jax.experimental import pallas as pl
from jax.experimental.pallas import tpu as pltpu
from jax.sharding import PartitionSpec as P

MODES = 6
GROUP = 8
AGG = 4
BS = 128
R = 32
K = 8
S = 16
C = 24
OMEGA = 0.7
BLOCK = S * K * MODES + GROUP
T_ENTRIES = R + 8 * S
UNROLL = 16
ROWS = 4
SMOOTH = 32
LIST = 384
LISTS = K + 2
NT = (((1,), (1,)), ((), ()))
VMEM = pl.BlockSpec(memory_space=pltpu.VMEM)
SMEM = pl.BlockSpec(memory_space=pltpu.SMEM)
HBM = pl.BlockSpec(memory_space=pltpu.HBM)


def params(mib):
    return pltpu.CompilerParams(vmem_limit_bytes=mib * 2**20)


def split(value):
    high = value.astype(jnp.bfloat16)
    return high, (value - high.astype(jnp.float32)).astype(jnp.bfloat16)


def pair_near(block, axis):
    return lax.ppermute(block, axis, [(i, i ^ 1) for i in range(lax.axis_size(axis))])


def pair_far(block, axis):
    pairs = [(i, i + 1) if i % 2 else (i, i - 1) for i in range(1, lax.axis_size(axis) - 1)]
    return lax.ppermute(block, axis, pairs)


def pair_halo(block, axis):
    far = pair_far(block, axis)
    return pair_near(block, axis), far


def pack_kernel(
    send_hbm, aggregate_hbm, modes_hbm, slab, column, live, own, message, raw, rows,
    send, aggregate, modes, sems
):
    copies = [
        pltpu.make_async_copy(source, target, sems.at[i])
        for i, (source, target) in enumerate(
            (
                (modes_hbm, modes),
                (aggregate_hbm, aggregate),
                (send_hbm, send),
                (slab, raw.at[0]),
                (column, raw.at[1]),
                (live, raw.at[2]),
            )
        )
    ]
    for copy in copies:
        copy.start()
    for copy in copies:
        copy.wait()
    for b in range(R):
        for m in range(MODES):
            own[b, m] = modes[m, b]
        own[b, MODES] = jnp.full((BS,), aggregate[b].astype(jnp.float32))
        own[b, MODES + 1] = jnp.zeros((BS,), jnp.float32)
    lane = lax.broadcasted_iota(jnp.int32, (1, BS), 1)
    sent = jnp.zeros((1, BS), jnp.int32)
    offered = jnp.zeros((1, BS), jnp.int32)
    for s in range(S):
        message[s] = own[send[s]]
        sent = jnp.where(lane == s, send[s], sent)
        offered = jnp.where(lane == send[s], 1, offered)
    rows[...] = jnp.concatenate([sent, offered, jnp.zeros((6, BS), jnp.int32)], 0)


def plan_kernel(where, raw, rows_ref, plan, wide):
    wide_odd, narrow_odd = where[0], where[1]
    wide[...] = jnp.zeros_like(wide)
    wide[:, :, 0:R] = raw[...]
    window, col, used = wide[0], wide[1], wide[2]
    window_row = (window * 11) >> 5
    down, across = window_row - 1, window - 3 * window_row - 1
    is_near, is_far = down == 1 - 2 * wide_odd, down == 2 * wide_odd - 1
    side = jnp.where(across == 0, 2, jnp.where(across == 1 - 2 * narrow_odd, 1, 0))
    block = side + jnp.where(is_near, 7, jnp.where(is_far, 4, 2))
    source = jnp.where(window == 4, col, block * S + col)
    kind = jnp.where(used == 0, 0, jnp.where(is_far & (across != 0), 2, 1))
    slot = lax.broadcasted_iota(jnp.int32, (K, BS), 0)
    lane = lax.broadcasted_iota(jnp.int32, (K, BS), 1)
    inside = lane < R
    entries = (
        (lane * K + slot)
        + (source << 8)
        + ((5 * window_row + across + 1) << 16)
        + (kind << 21)
        + (window << 23)
    )
    entries = jnp.where(inside, entries, 0)
    first = lane[0:1]
    sent, offered = rows_ref[0:1, :], rows_ref[1:2, :]
    is_live = (used != 0) & inside
    is_offered = jnp.broadcast_to(offered, (K, BS)) == 1
    before = (
        lax.broadcasted_iota(jnp.int32, (BS, BS), 0) < lax.broadcasted_iota(jnp.int32, (BS, BS), 1)
    ).astype(jnp.bfloat16)

    def counted(mask, even):
        ones = mask.astype(jnp.float32)
        ahead = [jnp.zeros((1, BS), jnp.float32)]
        for k in range(K):
            ahead.append(ahead[-1] + ones[k : k + 1])
        length = ahead.pop()
        if even:
            length = 2.0 * jnp.floor(0.5 * (length + 1.0))
        rows = jnp.broadcast_to(length, (K, BS))
        start = jnp.dot(rows.astype(jnp.bfloat16), before, preferred_element_type=jnp.float32)
        return start + jnp.concatenate(ahead, 0), jnp.sum(length, axis=1, keepdims=True)

    places, totals = [], []
    for rows in (is_offered, jnp.logical_not(is_offered)):
        top = is_live & rows & (slot == 0)
        other = is_live & rows & (slot != 0)
        place, _ = counted(top, False)
        place_other, total = counted(other, False)
        places.append((jnp.where(top, place, jnp.where(other, place_other + S, -1.0)), BS))
        totals.append(total + S)
    for i in (1, 2):
        mask = is_live & (kind == i)
        place, total = counted(mask, True)
        places.append((jnp.where(mask, place, -1.0), LIST))
        totals.append(total)
    choices = []
    for place, length in places:
        turned = place.T
        at = lax.broadcasted_iota(jnp.int32, (R, length), 1).astype(jnp.float32)
        choices.append(
            jnp.concatenate(
                [(turned[0:R, k : k + 1] == at).astype(jnp.bfloat16) for k in range(K)], 0
            )
        )
    rows = [
        jnp.concatenate([((entries >> (8 * i)) & 255)[k : k + 1, 0:R] for k in range(K)], 1)
        for i in range(4)
    ]
    rows.append(jnp.ones((1, K * R), jnp.int32))
    rows.append(jnp.zeros((11, K * R), jnp.int32))
    bytes_of = jnp.concatenate(rows, 0).astype(jnp.float32).astype(jnp.bfloat16)
    found = jnp.dot(
        bytes_of, jnp.concatenate(choices, 1), preferred_element_type=jnp.float32
    ).astype(jnp.int32)
    lists = found[0:1] + (found[1:2] << 8) + (found[2:3] << 16) + (found[3:4] << 24)
    filled = found[4:5] != 0
    plan[...] = jnp.zeros_like(plan)
    plan[0:K, 0:BS] = entries
    plan[K : K + 1, 0:BS] = sent
    numbers = jnp.where(first == 0, wide_odd, narrow_odd)
    for i, total in enumerate(totals):
        numbers = jnp.where(first == 2 + i, total.astype(jnp.int32), numbers)
    plan[K + 1 : K + 2, 0:BS] = numbers
    start = 0
    for i, ((_, length), block) in enumerate(zip(places, (0, 0, 0, 4))):
        part = slice(start, start + length)
        dummy = (25 << 16) + (block * S << 8)
        plan[LISTS + i : LISTS + i + 1, 0:length] = jnp.where(
            filled[:, part], lists[:, part], dummy
        )
        start += length


def pair_rows(high, low):
    zero = jnp.zeros_like(low)
    return jnp.concatenate(
        [jnp.concatenate([high, high], 1), jnp.concatenate([low, zero], 1)], 0
    )


def times_halves(value, halves):
    length = value.shape[0]
    both = lax.dot_general(
        pair_rows(*split(value)), halves, NT, preferred_element_type=jnp.float32
    )
    return both[:length] + both[length:]


def times_tile(value, tile):
    return times_halves(value, jnp.concatenate(split(tile), 1))


def scale_of(tile):
    eye = lax.broadcasted_iota(jnp.int32, (BS, BS), 0) == lax.broadcasted_iota(
        jnp.int32, (BS, BS), 1
    )
    diagonal = jnp.sum(jnp.where(eye, tile, 0.0), axis=0, keepdims=True)
    return jnp.broadcast_to(-OMEGA / diagonal, (GROUP, BS))


def member_marks(ints, table):
    source = (ints[0:K, 0:BS] >> 8) & 255

    def some(i, marks):
        for j in range(8):
            at = i * 8 + j
            marks = jnp.where(source == at, table[at, MODES : MODES + 1, :], marks)
        return marks

    return lax.fori_loop(0, T_ENTRIES // 8, some, jnp.zeros((K, BS), jnp.float32))


def coarse_marks(ints, members):
    return members + (((ints[0:K, 0:BS] >> 16) & 31) * AGG).astype(jnp.float32)


def fetch(tiles, entry, taken, at, sems):
    return pltpu.make_async_copy(tiles.at[entry & 255], taken.at[at], sems.at[at])


def start_batch(i, index, plan, tiles, taken, sems):
    for j in range(UNROLL):
        at = i * UNROLL + j
        pltpu.make_async_copy(
            tiles.at[plan[LISTS + index, at] & 255], taken.at[at], sems.at[i]
        ).start()


def wait_batch(i, tiles, taken, sems):
    at = pl.ds(i * UNROLL, UNROLL)
    pltpu.make_async_copy(tiles.at[pl.ds(0, UNROLL)], taken.at[at], sems.at[i]).wait()


def walk(index, plan, tiles, taken, sems, first, then):
    steps = (plan[K + 1, 2 + index] + UNROLL - 1) // UNROLL
    start_batch(0, index, plan, tiles, taken, sems)

    def start(i):
        @pl.when(i < steps)
        def _():
            start_batch(i, index, plan, tiles, taken, sems)

    start(1)
    start(2)
    wait_batch(0, tiles, taken, sems)
    first()
    for i in range(1, S * K // UNROLL):

        @pl.when(i < steps)
        def _(i=i):
            if i + 2 < S * K // UNROLL:
                start(i + 2)
            wait_batch(i, tiles, taken, sems)
            then(i)


def smooth_tiles(index, plan, tiles, table, slots, scale):
    count = plan[K + 1, 2 + index]
    for s in range(S):
        entry = plan[LISTS + index, s]
        at = entry & 255
        tile = tiles[at]
        modes = table[(entry >> 8) & 255]
        factor = scale_of(tile)
        scale[at // K] = factor
        slots[at] = times_tile(modes, tile) * factor + modes

    def some(i, carry):
        for j in range(SMOOTH):
            entry = plan[LISTS + index, jnp.minimum(S + i * SMOOTH + j, count - 1)]
            at = entry & 255
            value = times_tile(table[(entry >> 8) & 255], tiles[at])
            slots[at] = value * scale[at // K]
        return carry

    lax.fori_loop(0, (count - S + SMOOTH - 1) // SMOOTH, some, 0)


def bring_kernel(plan, tiles, halves, scale, taken, sems):
    def first():
        for s in range(S):
            tile = taken[s]
            scale[(plan[LISTS, s] & 255) // K] = scale_of(tile)
            halves[s] = jnp.concatenate(split(tile), 1)

    def then(i):
        for j in range(UNROLL):
            at = i * UNROLL + j
            halves[at] = jnp.concatenate(split(taken[at]), 1)

    walk(0, plan, tiles, taken, sems, first, then)


def offer_kernel(plan, ints, halves, scale, table, slots, message):
    count = plan[K + 1, 2]
    slots[...] = jnp.zeros_like(slots)
    marks = coarse_marks(ints, member_marks(ints, table))
    chosen = lax.broadcasted_iota(jnp.int32, (BS, BS), 0) == ints[K : K + 1, 0:BS]
    message[S * K * MODES :, :] = jnp.dot(
        marks, chosen.astype(jnp.float32), preferred_element_type=jnp.float32
    )

    def some(i, carry):
        for j in range(SMOOTH):
            place = jnp.minimum(i * SMOOTH + j, count - 1)
            entry = plan[LISTS, place]
            at = entry & 255
            modes = table[(entry >> 8) & 255]
            first = (at % K == 0).astype(jnp.float32)
            value = times_halves(modes, halves[place])
            slots[at] = value * scale[at // K] + first * modes
        return carry

    lax.fori_loop(0, (count + SMOOTH - 1) // SMOOTH, some, 0)
    for s in range(S):
        b = plan[K, s]
        for k in range(K):
            first = (s * K + k) * MODES
            message[first : first + MODES, :] = slots[b * K + k, :MODES]


def rest_kernel(
    plan, ints, tiles, table, begun, prolong_hbm, blocks, weights,
    prolong, slots, scale, marks, lab, dense_refs, sem, sems
):
    members = member_marks(ints, table)
    coarse = coarse_marks(ints, members)
    blocks[S * K * MODES : BLOCK, :] = coarse
    blocks[BLOCK + S * K * MODES :, :] = jnp.concatenate([coarse[:, S:], coarse[:, :S]], 1)
    marks[...] = members.astype(jnp.int32) + ((ints[0:K, 0:BS] >> 23) & 15) * AGG
    copy = pltpu.make_async_copy(marks, lab, sem)
    copy.start()
    slots[...] = begun[...]
    smooth_tiles(1, plan, tiles, table, slots, scale)
    copy.wait()

    def send_row(b):
        return pltpu.make_async_copy(prolong.at[b], prolong_hbm.at[b], sems.at[b])

    def rows(i, carry):
        for j, dense in enumerate(dense_refs):
            b = i * ROWS + j
            dense[...] = jnp.zeros_like(dense)
            for k in range(K):
                dense[lab[k, b]] += slots[b * K + k]
            for g in range(9 * AGG):
                prolong[b, MODES * g : MODES * (g + 1), :] = dense[g, :MODES]
            block, place = b // S, b % S
            start = pl.multiple_of(block * BLOCK + place * K * MODES, GROUP)
            own = jnp.concatenate([slots[b * K + k, :MODES] for k in range(K)], 0)
            blocks[pl.ds(start, K * MODES), :] = own
            high, low = split(prolong[b])
            weights[b, 0 : 9 * C, 0:BS] = high
            weights[b, 0 : 9 * C, BS:] = low
        for j in range(ROWS):
            send_row(i * ROWS + j).start()
        return carry

    lax.fori_loop(0, R // ROWS, rows, 0)

    def finish(b, carry):
        send_row(b).wait()
        return carry

    lax.fori_loop(0, R, finish, 0)


def couple_tiles(
    index, plan, first_block, tiles, weights, table, marks, lab, parts, products, last, totals, sem
):
    steps = jnp.maximum((plan[K + 1, 2 + index] + UNROLL - 1) // UNROLL, 2)
    for i in range(table.shape[0] // BLOCK):
        first = i * BLOCK + S * K * MODES
        marks[i * K : (i + 1) * K, :] = table[first : first + K, :].astype(jnp.int32)
    copy = pltpu.make_async_copy(marks, lab, sem)
    copy.start()
    length = K * MODES

    def apply_step(i, tiles_of=range(UNROLL)):
        for j in tiles_of:
            entry = plan[LISTS + index, i * UNROLL + j]
            source = (entry >> 8) & 255
            first = ((source >> 4) - first_block) * BLOCK + (source & 15) * length
            rows = table[pl.ds(pl.multiple_of(first, GROUP), length), :]
            high, low = split(times_tile(rows, tiles[entry & 255]))
            parts[length * j : length * (j + 1), :] = jnp.concatenate([high, low, high], 1)

    def product_step(i, products=products, tiles_of=range(UNROLL)):
        for j in tiles_of[::2]:
            b = (plan[LISTS + index, i * UNROLL + j] & 255) // K
            both = weights[b]
            at = slice(j * length, (j + 2) * length)
            products[at, :] = lax.dot_general(
                parts[at, :],
                jnp.concatenate([both[:, :BS], both], 1),
                NT,
                preferred_element_type=jnp.float32,
            )

    def place_step(i, products=products, tiles_of=range(UNROLL)):
        for j in tiles_of:
            entry = plan[LISTS + index, i * UNROLL + j]
            source = (entry >> 8) & 255
            shift = ((entry >> 16) & 31) * AGG
            major, minor = ((source >> 4) - first_block) * K, source & 15
            for g in range(K):
                at = (K * j + g) * MODES
                totals[g % 2][lab[major + g, minor] + shift] += products[at : at + GROUP, :]

    apply_step(0)
    product_step(0)
    apply_step(1)
    copy.wait()

    def step(i, carry):
        for j in range(0, UNROLL, 4):
            some = range(j, j + 4)
            place_step(i - 2, tiles_of=some)
            product_step(i - 1, tiles_of=some)
            apply_step(i, tiles_of=some)
        return carry

    lax.fori_loop(2, steps, step, 0)
    product_step(steps - 1, last)
    place_step(steps - 2)
    place_step(steps - 1, last)


def beside_kernel(
    plan, tiles, weights, table, out, marks, lab, parts, products, last, totals, sem
):
    for part in totals:
        part[0 : 25 * AGG] = jnp.zeros((25 * AGG, GROUP, 256), jnp.float32)
    couple_tiles(
        2, plan, 0, tiles, weights, table, marks, lab, parts, products, last, totals, sem
    )
    out[...] = totals[0][0 : 25 * AGG] + totals[1][0 : 25 * AGG]


def corner_kernel(
    plan, tiles, weights, begun, table, own_out, near_out, far_out,
    marks, lab, parts, products, last, totals, turned, sem
):
    totals[0][0 : 25 * AGG] = begun[...]
    totals[1][0 : 25 * AGG] = jnp.zeros((25 * AGG, GROUP, 256), jnp.float32)
    couple_tiles(
        3, plan, 4, tiles, weights, table, marks, lab, parts, products, last, totals, sem
    )
    for g in range(25 * AGG):
        turned[MODES * g : MODES * (g + 1), :] = totals[0][g, :MODES, :] + totals[1][g, :MODES, :]
    flat = turned[...].T
    even = plan[K + 1, 0] == 0
    low, mid, top = (flat[3 * C * i : 3 * C * (i + 1)] for i in range(3))
    own_out[...] = mid
    near_out[...] = jnp.where(even, top, low)
    far_out[...] = jnp.where(even, low, top)


def merge_kernel(where, blocks, own_out, near_out, far_out):
    even = where[0] == 0
    span = 5 * C
    mid, near, far = (blocks[3 * C * i : 3 * C * (i + 1), :] for i in range(3))
    low = jnp.where(even, near, far)
    top = jnp.where(even, far, near)
    zeros = jnp.zeros((3 * C, span), jnp.float32)
    length = 5 * span
    summed = (
        jnp.concatenate([top[:, :length], zeros, zeros], 1)
        + jnp.concatenate([zeros, mid[:, :length], zeros], 1)
        + jnp.concatenate([zeros, zeros, low[:, :length]], 1)
    )
    even = where[1] == 0
    low, mid, top = (summed[C * i : C * (i + 1)] for i in range(3))
    own_out[...] = mid
    near_out[...] = jnp.where(even, top, low)
    far_out[...] = jnp.where(even, low, top)


def place_kernel(where, own, near, far, coarse):
    even = where[1] == 0
    low = jnp.where(even, near[...], far[...])
    top = jnp.where(even, far[...], near[...])
    mid = own[...]
    zeros = jnp.zeros((C, C), jnp.float32)
    pieces = []
    for u in range(7):
        lanes = slice(5 * C * u, 5 * C * (u + 1))
        pieces.append(
            jnp.concatenate([top[:, lanes], zeros, zeros], 1)
            + jnp.concatenate([zeros, mid[:, lanes], zeros], 1)
            + jnp.concatenate([zeros, zeros, low[:, lanes]], 1)
        )
    coarse[...] = jnp.concatenate(pieces, 1)


def shape(*dims, dtype=jnp.float32):
    return jax.ShapeDtypeStruct(dims, dtype)


def body(operator_tiles, tile_slab, tile_column, tile_live, send_list, aggregate, null_modes):
    tiles = operator_tiles[0, 0]
    slab = tile_slab[0, 0].T
    column = tile_column[0, 0].T
    live = tile_live[0, 0].T
    send = send_list[0, 0]
    wide_odd = lax.axis_index("wide") % 2
    narrow_odd = lax.axis_index("narrow") % 2
    where = jnp.stack([wide_odd, narrow_odd]).astype(jnp.int32)

    own_modes, offered, raw, rows = pl.pallas_call(
        pack_kernel,
        out_shape=(
            shape(R, GROUP, BS),
            shape(S, GROUP, BS),
            shape(3, K, R, dtype=jnp.int32),
            shape(8, BS, dtype=jnp.int32),
        ),
        in_specs=[HBM] * 6,
        out_specs=(VMEM,) * 4,
        scratch_shapes=[
            pltpu.SMEM((S,), jnp.int32),
            pltpu.SMEM((R,), jnp.int32),
            pltpu.VMEM((MODES, R, BS), jnp.float32),
            pltpu.SemaphoreType.DMA((6,)),
        ],
        compiler_params=params(4),
        name="pack",
    )(
        *(
            pltpu.with_memory_space_constraint(x, pltpu.HBM)
            for x in (
                send, aggregate[0, 0], null_modes[0, 0].transpose(1, 0, 2), slab, column, live
            )
        )
    )
    near, far = pair_halo(offered, "narrow")
    plan = pl.pallas_call(
        plan_kernel,
        out_shape=shape(16, LIST, dtype=jnp.int32),
        in_specs=[SMEM] + [VMEM] * 2,
        out_specs=VMEM,
        scratch_shapes=[pltpu.VMEM((3, K, BS), jnp.int32)],
        compiler_params=params(8),
        cost_estimate=pl.CostEstimate(flops=10**8, bytes_accessed=5 * 10**6, transcendentals=0),
        name="plan",
    )(where, raw, rows)
    line = jnp.concatenate([far, near, offered], 0)
    line, plan = lax.optimization_barrier((line, plan))
    wide_near, wide_far = pair_halo(line, "wide")
    table = jnp.concatenate([own_modes, far, near, wide_far, wide_near], 0)

    tiles = tiles.reshape(R * K, BS, BS)
    resting = pltpu.with_memory_space_constraint(tiles, pltpu.HBM)
    taken = pltpu.VMEM((S * K, BS, BS), jnp.float32)
    scales = pltpu.VMEM((R, GROUP, BS), jnp.float32)
    halves, offered_scale = pl.pallas_call(
        bring_kernel,
        out_shape=(shape(S * K, BS, 2 * BS, dtype=jnp.bfloat16), shape(R, GROUP, BS)),
        in_specs=[SMEM, HBM],
        out_specs=(VMEM, VMEM),
        scratch_shapes=[taken, pltpu.SemaphoreType.DMA((S * K // UNROLL,))],
        compiler_params=params(24),
        cost_estimate=pl.CostEstimate(flops=10**8, bytes_accessed=10**7, transcendentals=0),
        name="bring",
    )(plan, resting)
    begun, message = pl.pallas_call(
        offer_kernel,
        out_shape=(shape(R * K, GROUP, BS), shape(BLOCK, BS)),
        in_specs=[SMEM, VMEM, VMEM, VMEM, VMEM],
        out_specs=(VMEM, VMEM),
        compiler_params=params(16),
        cost_estimate=pl.CostEstimate(flops=10**8, bytes_accessed=4 * 10**7, transcendentals=0),
        name="offer",
    )(plan, plan, halves, offered_scale, table)

    narrow_near, narrow_far = pair_halo(message, "narrow")
    wide_own = pair_far(message, "wide")
    prolong, blocks, weights = pl.pallas_call(
        rest_kernel,
        out_shape=(
            shape(R, 9 * C, BS),
            shape(2 * BLOCK, BS),
            shape(R, 256, 2 * BS, dtype=jnp.bfloat16),
        ),
        in_specs=[SMEM, VMEM, VMEM, VMEM, VMEM],
        out_specs=(HBM, VMEM, VMEM),
        scratch_shapes=[
            pltpu.VMEM((R, 9 * C, BS), jnp.float32),
            pltpu.VMEM((R * K, GROUP, BS), jnp.float32),
            scales,
            pltpu.VMEM((K, BS), jnp.int32),
            pltpu.SMEM((K, BS), jnp.int32),
            [pltpu.VMEM((9 * AGG, GROUP, BS), jnp.float32)] * ROWS,
            pltpu.SemaphoreType.DMA,
            pltpu.SemaphoreType.DMA((R,)),
        ],
        compiler_params=params(24),
        cost_estimate=pl.CostEstimate(flops=2 * 10**9, bytes_accessed=2 * 10**7, transcendentals=0),
        name="rest",
    )(plan, plan, tiles, table, begun)
    sides = jnp.concatenate([narrow_far, narrow_near], 0)
    line = jnp.concatenate([narrow_far, narrow_near, message], 0)
    line, sides, weights, wide_own = lax.optimization_barrier((line, sides, weights, wide_own))
    wide_near = pair_near(line, "wide")
    wide_far = pair_far(sides, "wide")

    def coupling(blocks):
        return [
            pltpu.VMEM((blocks * K, BS), jnp.int32),
            pltpu.SMEM((blocks * K, BS), jnp.int32),
            pltpu.VMEM((UNROLL * K * MODES, 3 * BS), jnp.bfloat16),
            pltpu.VMEM((UNROLL * K * MODES + GROUP, 256), jnp.float32),
            pltpu.VMEM((UNROLL * K * MODES + GROUP, 256), jnp.float32),
            [pltpu.VMEM((25 * AGG + 52, GROUP, 256), jnp.float32)] * 2,
        ]

    table = jnp.concatenate([blocks, sides, sides, wide_own, wide_near], 0)
    total = pl.pallas_call(
        beside_kernel,
        out_shape=shape(25 * AGG, GROUP, 256),
        in_specs=[SMEM] + [VMEM] * 3,
        out_specs=VMEM,
        scratch_shapes=coupling(10) + [pltpu.SemaphoreType.DMA],
        compiler_params=params(16),
        cost_estimate=pl.CostEstimate(flops=8 * 10**9, bytes_accessed=3 * 10**7, transcendentals=0),
        name="beside",
    )(plan, tiles, weights, table)
    own, near, far = pl.pallas_call(
        corner_kernel,
        out_shape=(shape(3 * C, 25 * C),) * 3,
        in_specs=[SMEM] + [VMEM] * 4,
        out_specs=(VMEM,) * 3,
        scratch_shapes=coupling(2)
        + [pltpu.VMEM((25 * C, 256), jnp.float32), pltpu.SemaphoreType.DMA],
        compiler_params=params(16),
        name="corner",
    )(plan, tiles, weights, total, wide_far)

    size = lax.axis_size("wide")
    pairs = [(i, i ^ 1) for i in range(size)]
    far_pairs = [(i, i + 1) if i % 2 else (i, i - 1) for i in range(1, size - 1)]
    near, far = lax.ppermute(near, "wide", pairs), lax.ppermute(far, "wide", far_pairs)
    own, near, far = pl.pallas_call(
        merge_kernel,
        out_shape=(shape(C, 35 * C),) * 3,
        in_specs=[SMEM, VMEM],
        out_specs=(VMEM,) * 3,
        compiler_params=params(4),
        name="merge",
    )(where, jnp.concatenate([own, near, far], 0))
    size = lax.axis_size("narrow")
    pairs = [(i, i ^ 1) for i in range(size)]
    far_pairs = [(i, i + 1) if i % 2 else (i, i - 1) for i in range(1, size - 1)]
    near, far = lax.ppermute(near, "narrow", pairs), lax.ppermute(far, "narrow", far_pairs)
    coarse = pl.pallas_call(
        place_kernel,
        out_shape=shape(C, 49 * C),
        in_specs=[SMEM] + [VMEM] * 3,
        out_specs=VMEM,
        compiler_params=params(4),
        name="place",
    )(where, own, near, far)
    return prolong[None, None], coarse[None, None]


def solution(mesh):
    in_specs = (
        P("wide", "narrow", None, None, None, None),
        P("wide", "narrow", None, None),
        P("wide", "narrow", None, None),
        P("wide", "narrow", None, None),
        P("wide", "narrow", None),
        P("wide", "narrow", None),
        P("wide", "narrow", None, None, None),
    )
    out_specs = (P("wide", "narrow", None, None, None), P("wide", "narrow", None, None))
    return jax.shard_map(body, mesh=mesh, in_specs=in_specs, out_specs=out_specs, check_vma=False)
```
